32 devices in a mesh: row: 4 (over y, x), col: 8 (over z, core).
Axes of the slice: x: 2, y: 2, z: 4, core: 2. Of those that a mesh axis runs over, the one named last changes fastest.
Arguments:
- coefficients: float32 [1024, 2048], P('row', 'col'), may hold values from -6 to 6
- diagonal: float32 [1024, 2048], P('row', 'col'), may hold values from 1.5 to 6
- energy_shift: float32 [1], replicated, may hold values from -1 to 0
- integrals: float32 [484, 484], replicated, may hold values from -0.25 to 0.25
- source_row: int32 [16, 512], P('row'), may hold values from 0 to 255
- target_row: int32 [16, 512], P('row'), may hold values from 0 to 7743
- phase_row: int32 [16, 512], P('row'), may hold values from -1 to 1, as said below
- source_col: int32 [64, 256], P('col'), may hold values from 0 to 255
- target_col: int32 [64, 256], P('col'), may hold values from 0 to 7743
- phase_col: int32 [64, 256], P('col'), may hold values from -1 to 1, as said below
Outputs:
- sigma_vector: float32 [1024, 2048], P('row', 'col')
- correction: float32 [1024, 2048], P('row', 'col')
The draws below stay inside these ranges and needn't reach their ends.
Inputs may be any that keep to these rules, and one draw needn't show every extreme that they name: `phase_row`: in each list row the entries with sign -1 or 1 come first and the rest are 0; in every draw some owner block receives all 512 slots live from every alpha block. `phase_col`: in each list row the entries with sign -1 or 1 come first and the rest are 0; in every draw some owner block receives all 256 slots live from every beta block.
All inputs are finite; a program needn't handle non-finite values.
Results may differ from the reference program's by a relative error of at most 0.000055.
Values sent between devices are 32-bit elements; how exact they have to be, the bound alone decides.
No kernel may reach another device: no remote copies, remote signals or barrier semaphores. Data moves between devices by JAX's collectives and lax.ppermute only.
A program may use at most 64 MiB of HBM per device.

```python
import jax
import jax.numpy as jnp
from jax import lax

PAIRS = 484
ROWS_A = 256
COLS_B = 256
K_DEV = 16
CAP_A = 512
CAP_B = 256
NA = 1024
NB = 2048
N_ROW = 4
N_COL = 8


def live_phases(key, dev_count, capacity):
    key_full, key_level, key_sign = jax.random.split(key, 3)
    full_owner = jax.random.randint(key_full, (), 0, dev_count)
    levels = jax.random.randint(key_level, (dev_count, dev_count), 6, 17)
    owners = jnp.arange(dev_count)[None, :]
    levels = jnp.where(owners == full_owner, 16, levels)
    counts = capacity * levels // 16
    slot_ids = jnp.arange(capacity)[None, None, :]
    live = (slot_ids < counts[:, :, None]).astype(jnp.int32)
    signs = 2 * jax.random.randint(key_sign, (dev_count, dev_count, capacity), 0, 2) - 1
    return (live * signs).reshape(dev_count * dev_count, capacity).astype(jnp.int32)


def draw_phase_row(key, part):
    return live_phases(jax.random.fold_in(key, 11), N_ROW, CAP_A)


def draw_phase_col(key, part):
    return live_phases(jax.random.fold_in(key, 23), N_COL, CAP_B)


def with_ends(entries, key, low, top_value):
    shape = entries.shape
    index_at = [jax.random.randint(jax.random.fold_in(key, axis), (), 0, shape[axis]) for axis in range(len(shape))]
    entries = entries.at[tuple(index_at)].set(low)
    longest = shape.index(max(shape))
    index_at[longest] = (index_at[longest] + 1) % shape[longest]
    return entries.at[tuple(index_at)].set(top_value)


def block_levels(stream_key, dims, cuts, smallest, largest):
    gain = 1.0
    for dim, blocks in cuts:
        steps = jax.random.uniform(jax.random.fold_in(jax.random.fold_in(stream_key, 6), dim), (blocks,), jnp.float32, smallest / len(cuts), largest / len(cuts))
        gain = gain * jnp.repeat(jnp.exp(steps), dims[dim] // blocks).reshape((-1,) + (1,) * (len(dims) - 1 - dim))
    return gain


def noise(rng, dims, scale, reach, pieces=(), kind=jnp.bfloat16):
    entries = jax.random.normal(rng, dims, jnp.float32) * scale
    if len(pieces) > 0:
        entries = block_levels(rng, dims, pieces, -0.22, 0.18) * entries
    return jnp.clip(entries, min=-reach, max=reach).astype(kind)


def setup_inputs(seed: int = 0) -> dict:
    seeds = jax.random.split(jax.random.key(seed), 11)
    return {
        "coefficients": noise(seeds[0], (NA, NB), 1.0, 6.0, ((0, 4), (1, 8)), jnp.float32),
        "diagonal": jnp.clip(1.5 + 4.5 * jax.random.uniform(seeds[1], (NA, NB), jnp.float32) ** block_levels(seeds[1], (NA, NB), ((0, 4), (1, 8)), -0.2, 0.2), 1.5, 6.0),
        "energy_shift": jnp.clip(jax.random.uniform(seeds[2], (1,), jnp.float32, -1.0, 0.0), -1.0, 0.0),
        "integrals": noise(seeds[3], (PAIRS, PAIRS), PAIRS ** -0.5, 0.25, (), jnp.float32),
        "source_row": with_ends(jax.random.randint(seeds[4], (N_ROW * N_ROW, CAP_A), 0, ROWS_A), jax.random.fold_in(seeds[4], 1), 0, ROWS_A - 1).astype(jnp.int32),
        "target_row": with_ends(jax.random.randint(seeds[5], (N_ROW * N_ROW, CAP_A), 0, K_DEV * PAIRS), jax.random.fold_in(seeds[5], 1), 0, (K_DEV * PAIRS) - 1).astype(jnp.int32),
        "phase_row": draw_phase_row(jax.random.fold_in(seeds[10], 71), 0),
        "source_col": with_ends(jax.random.randint(seeds[7], (N_COL * N_COL, CAP_B), 0, COLS_B), jax.random.fold_in(seeds[7], 1), 0, COLS_B - 1).astype(jnp.int32),
        "target_col": with_ends(jax.random.randint(seeds[8], (N_COL * N_COL, CAP_B), 0, K_DEV * PAIRS), jax.random.fold_in(seeds[8], 1), 0, (K_DEV * PAIRS) - 1).astype(jnp.int32),
        "phase_col": draw_phase_col(jax.random.fold_in(seeds[10], 71), 0),
    }


def same_spin(matrix, source, target, phases, dev_count, rows_dev, block_cols, block_count, integrals):
    total_rows = matrix.shape[0]
    pair_count = integrals.shape[0]
    list_index = jnp.arange(dev_count * dev_count).astype(jnp.int32)
    owner = list_index % dev_count
    sender = list_index // dev_count
    global_row = (sender[:, None] * rows_dev + source).reshape(-1).astype(jnp.int32)
    slot_index = (owner[:, None] * (K_DEV * pair_count) + target).reshape(-1).astype(jnp.int32)
    signs = phases.reshape(-1).astype(jnp.float32)

    def one_block(index):
        columns = lax.dynamic_slice_in_dim(matrix, index * block_cols, block_cols, 1)
        signed = columns[global_row] * signs[:, None]
        densities = jnp.zeros((dev_count * K_DEV * pair_count, block_cols), jnp.float32).at[slot_index].add(signed)
        products = jnp.einsum("ip,kpb->kib", integrals, densities.reshape(-1, pair_count, block_cols),
                              precision=lax.Precision.HIGHEST).reshape(-1, block_cols)
        picked = products[slot_index] * signs[:, None]
        return jnp.zeros((total_rows, block_cols), jnp.float32).at[global_row].add(picked)

    blocks = lax.map(one_block, jnp.arange(block_count).astype(jnp.int32))
    return jnp.transpose(blocks, (1, 0, 2)).reshape(total_rows, block_count * block_cols)


def reference(coefficients, diagonal, energy_shift, integrals, source_row, target_row, phase_row, source_col, target_col, phase_col):
    alpha_part = same_spin(coefficients, source_row, target_row, phase_row, N_ROW, ROWS_A, COLS_B, N_COL, integrals)
    beta_part = same_spin(coefficients.T, source_col, target_col, phase_col, N_COL, COLS_B, ROWS_A, N_ROW, integrals)
    sigma_vector = alpha_part + beta_part.T
    correction = (sigma_vector - energy_shift[0] * coefficients) / (diagonal - energy_shift[0])
    return sigma_vector, correction
```

```python
import functools

import jax
import jax.numpy as jnp
from jax import lax
from jax.experimental import pallas as pl
from jax.experimental.pallas import tpu as pltpu
from jax.sharding import PartitionSpec as P

BF16 = jnp.bfloat16
F32 = jnp.float32
NN = (((1,), (0,)), ((), ()))
NT = (((1,), (1,)), ((), ()))


def dot(x, y, dims=NN):
    return lax.dot_general(x, y, dims, preferred_element_type=F32)


def halves(x):
    high = x.astype(BF16)
    return high, (x - high.astype(F32)).astype(BF16)


def slot_of(place, pairs):
    return jnp.floor((place.astype(F32) + 0.5) * (1.0 / pairs)).astype(jnp.int32)


def one_hot(index, values, shape, axis):
    hit = lax.broadcasted_iota(jnp.int32, shape, axis) == index
    return jnp.where(hit, values, 0.0).astype(BF16)


def string_matrix_kernel(
    pairs, blocks, columns_ref, source_ref, other_ref, integrals_ref, out_ref, high_ref, low_ref
):
    owners, slots = source_ref.shape
    rows = out_ref.shape[0]
    width = out_ref.shape[1] // blocks
    depth = integrals_ref.shape[0]
    high, low = halves(integrals_ref[...])
    high_ref[...] = high
    low_ref[...] = low
    sums = [jnp.zeros((rows, width), F32) for _ in range(blocks)]
    for owner in range(owners):
        place = columns_ref[:, owner : owner + 1]
        sign = columns_ref[:, owners + owner : owners + owner + 1].astype(F32)
        slot = slot_of(place, pairs)
        pick = one_hot(place - slot * pairs, sign, (slots, depth), 1)
        rows_of_pairs = jnp.concatenate([dot(pick, high_ref[...]), dot(pick, low_ref[...])], axis=0).astype(BF16)
        spread = one_hot(source_ref[owner : owner + 1, :], 1.0, (rows, slots), 0)
        for block in range(blocks):
            at = block * owners + owner
            source2 = other_ref[0, at : at + 1, :]
            place2 = other_ref[1, at : at + 1, :]
            sign2 = other_ref[2, at : at + 1, :].astype(F32)
            slot2 = slot_of(place2, pairs)
            pick2 = one_hot(place2 - slot2 * pairs, sign2, (depth, slots), 0)
            entries = dot(rows_of_pairs, pick2)
            same = slot == slot2
            entries = jnp.concatenate(
                [jnp.where(same, entries[:slots], 0.0), jnp.where(same, entries[slots:], 0.0)], axis=0
            ).astype(BF16)
            gather2 = one_hot(source2, 1.0, (width, slots), 0)
            half = dot(entries, gather2, NT)
            top, rest = halves(half[:slots] + half[slots:])
            sums[block] += dot(spread, top) + dot(spread, rest)
    for block in range(blocks):
        out_ref[:, block * width : (block + 1) * width] = sums[block]


def string_matrix(own, other, integrals, pairs, rows, width):
    owners, slots = own.shape[1:]
    blocks = other.shape[1]
    depth = integrals.shape[0]
    columns = own[1:].reshape(2 * owners, slots).T
    flops = 2 * owners * 2 * (
        slots * depth * depth + blocks * (slots * depth * slots + slots * slots * width + rows * slots * width)
    )
    return pl.pallas_call(
        functools.partial(string_matrix_kernel, pairs, blocks),
        out_shape=jax.ShapeDtypeStruct((rows, blocks * width), F32),
        in_specs=[pl.BlockSpec(memory_space=pltpu.VMEM)] * 4,
        out_specs=pl.BlockSpec(memory_space=pltpu.VMEM),
        scratch_shapes=[pltpu.VMEM((depth, depth), BF16)] * 2,
        compiler_params=pltpu.CompilerParams(vmem_limit_bytes=40 << 20),
        cost_estimate=pl.CostEstimate(flops=flops, bytes_accessed=4 << 20, transcendentals=0),
    )(columns, own[0], other.reshape(3, blocks * owners, slots), integrals)


def final_kernel(count, nb, index_ref, *refs):
    at = iter(refs)
    take = lambda n: [next(at) for _ in range(n)]
    c_row = take(count)
    h_a = [take(nb) for _ in range(count)]
    c_col = [take(nb) for _ in range(count)]
    h_b = take(count)
    diagonal_ref, shift_ref = take(2)
    sigma_ref, correction_ref = take(2)
    row_high, row_low, col_high, col_low = take(4)
    rows, cols = sigma_ref.shape
    group, row = index_ref[0], index_ref[1]
    for d in range(count):
        row_high[d], row_low[d] = halves(c_row[d][...])
        for j in range(nb):
            col_high[d, j], col_low[d, j] = halves(c_col[d][j][...])
    total = jnp.zeros((rows, cols), F32)
    for d in range(count):
        parts = [halves(h_a[d][j][...]) for j in range(nb)]
        high = jnp.concatenate([p[0] for p in parts], axis=0)
        low = jnp.concatenate([p[1] for p in parts], axis=0)
        far = group ^ d
        total += dot(high, row_high[far]) + dot(high, row_low[far]) + dot(low, row_high[far])
        far = row ^ d
        for j in range(nb):
            high, low = halves(h_b[d][:, j * cols : (j + 1) * cols])
            total += dot(col_high[far, j], high, NT) + dot(col_low[far, j], high, NT) + dot(col_high[far, j], low, NT)
    shift = shift_ref[0]
    sigma_ref[...] = total
    correction_ref[...] = (total - shift * c_row[0][...]) / (diagonal_ref[...] - shift)


def final(group, row, c_row, h_a, c_col, h_b, diagonal, energy_shift):
    count, nb = len(c_row), len(c_col[0])
    rows, cols = diagonal.shape
    operands = [*c_row]
    for d in range(count):
        operands += h_a[d]
    for d in range(count):
        operands += c_col[d]
    operands += [*h_b, diagonal]
    vmem = pl.BlockSpec(memory_space=pltpu.VMEM)
    smem = pl.BlockSpec(memory_space=pltpu.SMEM)
    return pl.pallas_call(
        functools.partial(final_kernel, count, nb),
        out_shape=[jax.ShapeDtypeStruct((rows, cols), F32)] * 2,
        in_specs=[smem] + [vmem] * len(operands) + [smem],
        out_specs=[vmem] * 2,
        scratch_shapes=[pltpu.VMEM((count, rows, cols), BF16)] * 2 + [pltpu.VMEM((count, nb, rows, cols), BF16)] * 2,
        compiler_params=pltpu.CompilerParams(vmem_limit_bytes=48 << 20),
        cost_estimate=pl.CostEstimate(
            flops=6 * count * rows * cols * (rows + nb * cols), bytes_accessed=8 << 20, transcendentals=0
        ),
    )(jnp.stack([group, row]), *operands, energy_shift)


def shards(
    n_row,
    n_col,
    coefficients,
    diagonal,
    energy_shift,
    integrals,
    source_row,
    target_row,
    phase_row,
    source_col,
    target_col,
    phase_col,
):
    nb = n_col // n_row
    rows, cols = coefficients.shape
    pairs = integrals.shape[0]
    depth = -(-pairs // 256) * 256
    row, col = lax.axis_index("row"), lax.axis_index("col")
    group, member = col // nb, col % nb
    last = n_row - 1

    def groups(x, d):
        return lax.ppermute(x, "col", [(c, ((c // nb) ^ d) * nb + c % nb) for c in range(n_col)])

    def members(x, k):
        return lax.ppermute(x, "col", [((c // nb) * nb + (c % nb + k) % nb, c) for c in range(n_col)])

    def rows_of(x, d):
        return lax.ppermute(x, "row", [(r, r ^ d) for r in range(n_row)])

    def every(move, x):
        blocks = [x]
        for d in range(1, n_row):
            blocks.append(move(blocks[d & (d - 1)], d & -d))
        return blocks

    both = [(r, c) for r in range(n_row) for c in range(n_col)]

    def lists_a(x):
        return lax.ppermute(x, ("row", "col"), [((r ^ (c // nb)) * n_col + c, r * n_col + c) for r, c in both])

    def lists_b(x, d):
        return lax.ppermute(
            x, ("row", "col"), [(r * n_col + ((c // nb) ^ r ^ d) * nb + c % nb, r * n_col + c) for r, c in both]
        )

    alpha = jnp.stack([source_row, target_row, phase_row])
    beta = jnp.stack([source_col, target_col, phase_col])
    share = n_row // nb
    alpha = lax.dynamic_slice_in_dim(alpha, member * share, share, 1)
    alpha_far = lists_a(alpha)
    beta_near, beta_far = lists_b(beta, 0), lists_b(beta, last)
    pair_of = jnp.stack([beta_near, beta_far])
    swapped = [members(pair_of, k) for k in range(1, nb)]
    c_row = every(rows_of, coefficients)
    c_own = every(groups, coefficients)
    integrals = jnp.pad(integrals, ((0, depth - pairs), (0, depth - pairs)))

    def beta_blocks(which):
        by_shift = [pair_of[which]] + [s[which] for s in swapped]
        if nb == 1:
            return by_shift[0][:, None]
        blocks = jnp.stack(by_shift, axis=1)
        return jnp.roll(blocks, member, axis=1) if nb > 1 else blocks

    near = string_matrix(beta, beta_blocks(0), integrals, pairs, cols, cols)
    h_b = {0: near}
    for d in range(1, last):
        h_b[d] = rows_of(near, d)
    part = string_matrix(alpha, alpha_far[:, None], integrals, pairs, rows, rows)
    piece = rows // nb
    mine = lax.dynamic_slice_in_dim(part, member * piece, piece, 0)
    for k in range(1, nb):
        theirs = lax.dynamic_slice_in_dim(part, ((member + nb - k) % nb) * piece, piece, 0)
        mine = mine + members(theirs, k)
    a_blocks = every(groups, mine)
    a_stack = jnp.concatenate(a_blocks, axis=0)
    a_by_shift = [a_stack] + [members(a_stack, k) for k in range(1, nb)]
    h_b[last] = string_matrix(beta, beta_blocks(1), integrals, pairs, cols, cols)

    def by_member(shifted):
        if nb == 1:
            return shifted
        stacked = jnp.stack(shifted)
        rolled = jnp.roll(stacked, member, axis=0)
        return [rolled[j] for j in range(nb)]

    a_members = by_member(a_by_shift)
    h_a = [[a_members[j][d * piece : (d + 1) * piece] for j in range(nb)] for d in range(n_row)]
    c_stack = jnp.concatenate(c_own, axis=0)
    c_members = by_member([c_stack] + [members(c_stack, k) for k in range(1, nb)])
    c_col = [[c_members[j][d * rows : (d + 1) * rows] for j in range(nb)] for d in range(n_row)]
    return final(
        group, row, c_row, h_a, c_col, [h_b[d] for d in range(n_row)], diagonal, energy_shift
    )


def solution(mesh):
    n_row, n_col = mesh.shape["row"], mesh.shape["col"]
    in_specs = (
        P("row", "col"),
        P("row", "col"),
        P(),
        P(),
        P("row", None),
        P("row", None),
        P("row", None),
        P("col", None),
        P("col", None),
        P("col", None),
    )
    out_specs = (P("row", "col"), P("row", "col"))
    return jax.shard_map(
        functools.partial(shards, n_row, n_col), mesh=mesh, in_specs=in_specs, out_specs=out_specs, check_vma=False
    )
```

```python
import functools
import math

import jax
import jax.numpy as jnp
from jax import lax
from jax.experimental import pallas as pl
from jax.experimental.pallas import tpu as pltpu
from jax.sharding import PartitionSpec as P

BF16 = jnp.bfloat16
F32 = jnp.float32
NN = (((1,), (0,)), ((), ()))
NT = (((1,), (1,)), ((), ()))
VMEM = pl.BlockSpec(memory_space=pltpu.VMEM)
ANY = pl.BlockSpec(memory_space=pl.ANY)
SMEM = pl.BlockSpec(memory_space=pltpu.SMEM)


def dot(x, y, dims=NN):
    return lax.dot_general(x, y, dims, preferred_element_type=F32)


def halves(x):
    high = x.astype(BF16)
    return high, (x - high.astype(F32)).astype(BF16)


def slot_of(place, pairs):
    return jnp.floor((place + 0.5) * (1.0 / pairs))


def one_hot(index, values, shape, axis):
    hit = lax.broadcasted_iota(jnp.int32, shape, axis) == index.astype(jnp.int32)
    return jnp.where(hit, values, 0.0).astype(BF16)


def joined(parts, axis):
    return parts[0] if len(parts) == 1 else jnp.concatenate(parts, axis=axis)


def fetched(sources, targets, sems):
    copies = [pltpu.make_async_copy(x, y, sems.at[i]) for i, (x, y) in enumerate(zip(sources, targets, strict=True))]
    for copy in copies:
        copy.start()
    return copies


def string_matrix_kernel(pairs, where, per, outs, after, *refs):
    refs = iter(refs)
    columns_ref, source_ref, integrals_ref = (next(refs) for _ in range(3))
    other_refs = [next(refs) for _ in range(1 + max(array for array, _ in where))]
    for _ in range(after):
        next(refs)
    out_refs = [next(refs) for _ in range(outs)]
    lists_ref, picked_ref, one_hot_ref, spread_ref, left_ref, sems = refs
    blocks = len(where)
    owners, slots = source_ref.shape
    rows, width = out_refs[0].shape
    width = width * outs // blocks
    depth = picked_ref.shape[2]
    lanes = lists_ref.shape[2]
    sources = [other_refs[array].at[pl.ds(base, lists_ref.shape[1])] for array, base in where]
    copies = fetched(sources, [lists_ref.at[block] for block in range(blocks)], sems)

    def listed(block, kind, owner):
        at = (kind * owners + owner) * slots
        if slots <= lanes:
            return lists_ref[block, at // lanes : at // lanes + 1, at % lanes : at % lanes + slots]
        return jnp.concatenate(
            [lists_ref[block, r : r + 1, :] for r in range(at // lanes, (at + slots) // lanes)], axis=1
        )

    high, low = halves(integrals_ref[...])
    batch = one_hot_ref.shape[0] // slots
    for first in range(0, owners, batch):
        for i in range(batch):
            place = columns_ref[:, first + i : first + i + 1]
            sign = columns_ref[:, owners + first + i : owners + first + i + 1]
            pair = place - slot_of(place, pairs) * pairs
            one_hot_ref[i * slots : (i + 1) * slots] = one_hot(pair, sign, (slots, depth), 1)
        top = dot(one_hot_ref[...], high).astype(BF16)
        rest = dot(one_hot_ref[...], low).astype(BF16)
        for i in range(batch):
            picked_ref[first + i, :slots] = top[i * slots : (i + 1) * slots]
            picked_ref[first + i, slots:] = rest[i * slots : (i + 1) * slots]
    for owner in range(owners):
        spread = one_hot(source_ref[owner : owner + 1, :], 1.0, (rows, slots), 0)
        spread_ref[owner, :, :slots] = spread
        spread_ref[owner, :, slots:] = spread
    for copy in copies:
        copy.wait()
    for first in range(0, blocks, per):
        group = range(first, first + per)
        for owner in range(owners):
            slot = slot_of(columns_ref[:, owner : owner + 1], pairs)
            picks, slots2 = [], []
            for block in group:
                place2 = listed(block, 1, owner)
                slot2 = slot_of(place2, pairs)
                slots2.append(slot2)
                picks.append(one_hot(place2 - slot2 * pairs, listed(block, 2, owner), (depth, slots), 0))
            entries = dot(picked_ref[owner], joined(picks, 1))
            same = slot == joined(slots2, 1)
            entries = jnp.concatenate(
                [jnp.where(same, entries[:slots], 0.0), jnp.where(same, entries[slots:], 0.0)], axis=0
            ).astype(BF16)
            top, rest = halves(dot(spread_ref[owner], entries))
            for i in range(per):
                left_ref[i, :rows, owner * slots : (owner + 1) * slots] = top[:, i * slots : (i + 1) * slots]
                left_ref[i, rows:, owner * slots : (owner + 1) * slots] = rest[:, i * slots : (i + 1) * slots]
        for i, block in enumerate(group):
            gathers = [one_hot(listed(block, 0, owner), 1.0, (width, slots), 0) for owner in range(owners)]
            both = dot(left_ref[i], joined(gathers, 1), NT)
            out, at = divmod(block, blocks // outs)
            out_refs[out][:, at * width : (at + 1) * width] = both[:rows] + both[rows:]


def string_matrix(columns, source, integrals, others, where, pairs, rows, width, outs, after=()):
    owners, slots = source.shape
    blocks = len(where)
    depth = integrals.shape[0]
    per = max(1, min(blocks, 512 // slots))
    batch = max(1, min(owners, 1024 // slots))
    flops = 4 * owners * slots * (depth * depth + blocks * (depth * slots + rows * slots + rows * width))
    scratch = [
        (owners, 2 * slots, depth),
        (batch * slots, depth),
        (owners, rows, 2 * slots),
        (per, 2 * rows, owners * slots),
    ]
    scratch_bytes = 2 * sum(math.prod(shape) for shape in scratch)
    lanes = others[0].shape[1]
    list_rows = -(-3 * owners * slots // (8 * lanes)) * 8
    return pl.pallas_call(
        functools.partial(string_matrix_kernel, pairs, where, per, outs, len(after)),
        out_shape=[jax.ShapeDtypeStruct((rows, blocks // outs * width), F32)] * outs,
        in_specs=[VMEM] * 3 + [ANY] * (len(others) + len(after)),
        out_specs=[VMEM] * outs,
        scratch_shapes=[pltpu.VMEM((blocks, list_rows, lanes), F32)]
        + [pltpu.VMEM(shape, BF16) for shape in scratch]
        + [pltpu.SemaphoreType.DMA((blocks,))],
        compiler_params=pltpu.CompilerParams(vmem_limit_bytes=scratch_bytes + (6 << 20)),
        cost_estimate=pl.CostEstimate(flops=flops, bytes_accessed=1 << 10, transcendentals=0),
    )(columns, source, integrals, *others, *after)


def three_products(x, y, dims=NN):
    return dot(x[0], y[0], dims) + dot(x[0], y[1], dims) + dot(x[1], y[0], dims)


def beta_kernel(count, nb, index_ref, *refs):
    *refs, out_ref, c_ref, h_ref, sems = refs
    rows, cols = out_ref.shape
    targets = [*[c_ref.at[i] for i in range(count * nb)], *[h_ref.at[d] for d in range(count)]]
    copies = fetched(refs, targets, sems)
    for copy in copies[count * nb :]:
        copy.wait()
    row = index_ref[0]
    total = jnp.zeros((rows, cols), F32)
    for d in range(count):
        for k in range(nb):
            copies[d * nb + k].wait()
            right = halves(h_ref[row ^ d, :, k * cols : (k + 1) * cols])
            total += three_products(halves(c_ref[d * nb + k]), right, NT)
    out_ref[...] = total


def beta_part(index, c_col, h_b, rows, cols):
    count, nb = len(c_col), len(c_col[0])
    operands = [*sum(c_col, []), *h_b]
    return pl.pallas_call(
        functools.partial(beta_kernel, count, nb),
        out_shape=jax.ShapeDtypeStruct((rows, cols), F32),
        in_specs=[SMEM] + [ANY] * len(operands),
        out_specs=VMEM,
        scratch_shapes=[
            pltpu.VMEM((count * nb, rows, cols), F32),
            pltpu.VMEM((count, cols, nb * cols), F32),
            pltpu.SemaphoreType.DMA((count * nb + count,)),
        ],
        compiler_params=pltpu.CompilerParams(vmem_limit_bytes=4 * count * nb * cols * (rows + cols) + (6 << 20)),
        cost_estimate=pl.CostEstimate(
            flops=100 * count * nb * rows * cols * cols, bytes_accessed=1 << 10, transcendentals=0
        ),
    )(index, *operands)


def final_kernel(count, nb, shift_ref, *refs):
    *refs, sigma_ref, correction_ref, c_ref, h_ref, beta_ref, diagonal_ref, sems = refs
    rows, cols = sigma_ref.shape
    c_row, h_a, beta, diagonal = refs[:count], refs[count : count + nb], refs[-2], refs[-1]
    targets = [*[c_ref.at[d] for d in range(count)], *[h_ref.at[k] for k in range(nb)], beta_ref, diagonal_ref]
    copies = fetched([*[c.at[:rows] for c in c_row], *h_a, beta, diagonal], targets, sems)
    for copy in copies[count : count + nb]:
        copy.wait()
    total = jnp.zeros((rows, cols), F32)
    for d in range(count):
        copies[d].wait()
        left = h_ref[0, :, d * rows : (d + 1) * rows]
        for k in range(1, nb):
            left = left + h_ref[k, :, d * rows : (d + 1) * rows]
        total += three_products(halves(left), halves(c_ref[d]))
    for copy in copies[count + nb :]:
        copy.wait()
    shift = shift_ref[0]
    total += beta_ref[...]
    sigma_ref[...] = total
    correction_ref[...] = (total - shift * c_ref[0]) / (diagonal_ref[...] - shift)


def final(energy_shift, c_row, h_a, beta, diagonal):
    count, nb = len(c_row), len(h_a)
    rows, cols = diagonal.shape
    operands = [*c_row, *h_a, beta, diagonal]
    scratch = [(count, rows, cols), (nb, rows, count * rows), (rows, cols), (rows, cols)]
    return pl.pallas_call(
        functools.partial(final_kernel, count, nb),
        out_shape=[jax.ShapeDtypeStruct((rows, cols), F32)] * 2,
        in_specs=[SMEM] + [ANY] * len(operands),
        out_specs=[VMEM] * 2,
        scratch_shapes=[pltpu.VMEM(shape, F32) for shape in scratch]
        + [pltpu.SemaphoreType.DMA((len(operands),))],
        compiler_params=pltpu.CompilerParams(
            vmem_limit_bytes=4 * sum(math.prod(shape) for shape in scratch) + (6 << 20)
        ),
        cost_estimate=pl.CostEstimate(
            flops=100 * count * rows * rows * cols, bytes_accessed=1 << 10, transcendentals=0
        ),
    )(energy_shift, *operands)


def shards(
    n_row,
    n_col,
    coefficients,
    diagonal,
    energy_shift,
    integrals,
    source_row,
    target_row,
    phase_row,
    source_col,
    target_col,
    phase_col,
):
    nb = n_col // n_row
    rows, cols = coefficients.shape
    pairs = integrals.shape[0]
    depth = -(-pairs // 256) * 256
    row, col = lax.axis_index("row"), lax.axis_index("col")
    group, member = col // nb, col % nb
    last = n_row - 1

    def members(x, k):
        return lax.ppermute(x, "col", [((c // nb) * nb + (c % nb + k) % nb, c) for c in range(n_col)])

    def rows_of(x, d):
        return lax.ppermute(x, "row", [(r, r ^ d) for r in range(n_row)])

    def lists_of(x, d):
        pairs_of = [
            (r * n_col + ((c // nb) ^ r ^ d) * nb + c % nb, r * n_col + c) for r in range(n_row) for c in range(n_col)
        ]
        return lax.ppermute(x, ("row", "col"), pairs_of)

    def groups(x, d):
        return lax.ppermute(x, "col", [(c, ((c // nb) ^ d) * nb + c % nb) for c in range(n_col)])

    def every(move, x):
        blocks = {0: x}
        for d in sorted(range(1, n_row), key=lambda d: (d.bit_count(), -d)):
            blocks[d] = move(blocks[d & (d - 1)], d & -d)
        return [blocks[d] for d in range(n_row)]

    beta = jnp.concatenate([source_col, target_col, phase_col]).astype(F32)
    owners_b, slots_b = source_col.shape
    beta_both = jnp.concatenate([beta] + [members(beta, k) for k in range(1, nb)])
    beta_lists = [lists_of(beta_both, d) for d in (0, last)]
    where_b = [(i, k * 3 * owners_b) for i in range(2) for k in range(nb)]

    share = n_row // nb
    slots_a = source_row.shape[1]
    alpha = jnp.stack([source_row, target_row, phase_row]).astype(F32)
    alpha = lax.dynamic_slice_in_dim(alpha, member * share, share, 1)
    lists = alpha.reshape(-1, cols)
    lists = jnp.pad(lists, ((0, -lists.shape[0] % 8), (0, 0)))
    payload = jnp.concatenate([coefficients, lists], axis=0)
    c_row = [payload] + [rows_of(payload, d) for d in range(1, n_row)]
    where_a = [(d, rows) for d in range(n_row)]
    c_own = every(groups, coefficients)
    integrals = jnp.pad(integrals, ((0, depth - pairs), (0, depth - pairs)))

    beta_side = (beta[owners_b:].T, beta[:owners_b], integrals)
    near, far = string_matrix(*beta_side, beta_lists, where_b, pairs, cols, cols, 2)
    h_b = [near] + [rows_of(near, d) for d in range(1, last)] + [far]
    alpha_side = (alpha[1:].reshape(-1, slots_a).T, alpha[0], integrals)
    early = {d: c_own[d] for d in range(n_row) if d & (d - 1) == 0}
    swapped = {d: [members(block, k) for k in range(1, nb)] for d, block in early.items()}
    (part,) = string_matrix(*alpha_side, c_row, where_a, pairs, rows, rows, 1, [near, *early.values()])
    for d in range(n_row):
        if d not in swapped:
            swapped[d] = [members(c_own[d], k) for k in range(1, nb)]
    h_a = [part] + [members(part, k) for k in range(1, nb)]
    c_col = [[c_own[d], *swapped[d]] for d in range(n_row)]
    beta_sum = beta_part(row[None], c_col, h_b, rows, cols)
    return final(energy_shift, c_row, h_a, beta_sum, diagonal)


def solution(mesh):
    n_row, n_col = mesh.shape["row"], mesh.shape["col"]
    in_specs = (
        P("row", "col"),
        P("row", "col"),
        P(),
        P(),
        P("row", None),
        P("row", None),
        P("row", None),
        P("col", None),
        P("col", None),
        P("col", None),
    )
    out_specs = (P("row", "col"), P("row", "col"))
    return jax.shard_map(
        functools.partial(shards, n_row, n_col), mesh=mesh, in_specs=in_specs, out_specs=out_specs, check_vma=False
    )
```

```python
import functools
import math

import jax
import jax.numpy as jnp
from jax import lax
from jax.experimental import pallas as pl
from jax.experimental.pallas import tpu as pltpu
from jax.sharding import PartitionSpec as P

BF16 = jnp.bfloat16
F32 = jnp.float32
NN = (((1,), (0,)), ((), ()))
NT = (((1,), (1,)), ((), ()))
VMEM = pl.BlockSpec(memory_space=pltpu.VMEM)
ANY = pl.BlockSpec(memory_space=pl.ANY)
SMEM = pl.BlockSpec(memory_space=pltpu.SMEM)


def dot(x, y, dims=NN):
    return lax.dot_general(x, y, dims, preferred_element_type=F32)


def halves(x):
    high = x.astype(BF16)
    return high, (x - high.astype(F32)).astype(BF16)


def slot_of(place, pairs):
    return jnp.floor((place + 0.5) * (1.0 / pairs))


def one_hot(index, values, shape, axis):
    hit = lax.broadcasted_iota(jnp.int32, shape, axis) == index.astype(jnp.int32)
    return jnp.where(hit, values, 0.0).astype(BF16)


def joined(parts, axis):
    return parts[0] if len(parts) == 1 else jnp.concatenate(parts, axis=axis)


def fetched(sources, targets, sems):
    copies = [pltpu.make_async_copy(x, y, sems.at[i]) for i, (x, y) in enumerate(zip(sources, targets, strict=True))]
    for copy in copies:
        copy.start()
    return copies


def string_matrix_kernel(pairs, where, per, outs, after, member_ref, *refs):
    refs = iter(refs)
    columns_ref, source_ref, integrals_ref = (next(refs) for _ in range(3))
    other_refs = [next(refs) for _ in range(1 + max(array for array, _ in where[0]))]
    for _ in range(after):
        next(refs)
    out_refs = [next(refs) for _ in range(outs)]
    lists_ref, padded_ref, picked_ref, one_hot_ref, spread_ref, left_ref, sems = refs
    blocks = len(where[0])
    owners, slots = source_ref.shape
    rows, width = out_refs[0].shape
    width = width * outs // blocks
    depth = picked_ref.shape[2]
    lanes = lists_ref.shape[2]
    if len(where) == 1:
        sources = [other_refs[array].at[pl.ds(base, lists_ref.shape[1])] for array, base in where[0]]
        copies = fetched(sources, [lists_ref.at[block] for block in range(blocks)], sems)
    else:
        copies = []
        for block in range(blocks):
            choices = [other_refs[at[block][0]][pl.ds(at[block][1], lists_ref.shape[1])] for at in where]
            lists_ref[block] = jnp.where(member_ref[0] == 0, choices[0], choices[1])

    def listed(block, kind, owner):
        at = (kind * owners + owner) * slots
        if slots <= lanes:
            return lists_ref[block, at // lanes : at // lanes + 1, at % lanes : at % lanes + slots]
        return jnp.concatenate(
            [lists_ref[block, r : r + 1, :] for r in range(at // lanes, (at + slots) // lanes)], axis=1
        )

    padded_ref[...] = jnp.zeros(padded_ref.shape, F32)
    padded_ref[:pairs, :pairs] = integrals_ref[...]
    high, low = halves(padded_ref[...])
    batch = one_hot_ref.shape[0] // slots
    for first in range(0, owners, batch):
        for i in range(batch):
            place = columns_ref[:, first + i : first + i + 1]
            sign = columns_ref[:, owners + first + i : owners + first + i + 1]
            pair = place - slot_of(place, pairs) * pairs
            one_hot_ref[i * slots : (i + 1) * slots] = one_hot(pair, sign, (slots, depth), 1)
        top = dot(one_hot_ref[...], high).astype(BF16)
        rest = dot(one_hot_ref[...], low).astype(BF16)
        for i in range(batch):
            picked_ref[first + i, :slots] = top[i * slots : (i + 1) * slots]
            picked_ref[first + i, slots:] = rest[i * slots : (i + 1) * slots]
    for owner in range(owners):
        spread = one_hot(source_ref[owner : owner + 1, :], 1.0, (rows, slots), 0)
        spread_ref[owner, :, :slots] = spread
        spread_ref[owner, :, slots:] = spread
    for copy in copies:
        copy.wait()
    for first in range(0, blocks, per):
        group = range(first, first + per)
        for owner in range(owners):
            slot = slot_of(columns_ref[:, owner : owner + 1], pairs)
            picks, slots2 = [], []
            for block in group:
                place2 = listed(block, 1, owner)
                slot2 = slot_of(place2, pairs)
                slots2.append(slot2)
                picks.append(one_hot(place2 - slot2 * pairs, listed(block, 2, owner), (depth, slots), 0))
            entries = dot(picked_ref[owner], joined(picks, 1))
            same = slot == joined(slots2, 1)
            entries = jnp.concatenate(
                [jnp.where(same, entries[:slots], 0.0), jnp.where(same, entries[slots:], 0.0)], axis=0
            ).astype(BF16)
            top, rest = halves(dot(spread_ref[owner], entries))
            for i in range(per):
                left_ref[i, :rows, owner * slots : (owner + 1) * slots] = top[:, i * slots : (i + 1) * slots]
                left_ref[i, rows:, owner * slots : (owner + 1) * slots] = rest[:, i * slots : (i + 1) * slots]
        for i, block in enumerate(group):
            gathers = [one_hot(listed(block, 0, owner), 1.0, (width, slots), 0) for owner in range(owners)]
            both = dot(left_ref[i], joined(gathers, 1), NT)
            out, at = divmod(block, blocks // outs)
            out_refs[out][:, at * width : (at + 1) * width] = both[:rows] + both[rows:]


def string_matrix(member, columns, source, integrals, others, where, pairs, rows, width, outs, after=()):
    owners, slots = source.shape
    blocks = len(where[0])
    depth = -(-pairs // 256) * 256
    per = max(1, min(blocks, 512 // slots))
    batch = max(1, min(owners, 1024 // slots))
    flops = 4 * owners * slots * (depth * depth + blocks * (depth * slots + rows * slots + rows * width))
    scratch = [
        (owners, 2 * slots, depth),
        (batch * slots, depth),
        (owners, rows, 2 * slots),
        (per, 2 * rows, owners * slots),
    ]
    scratch_bytes = 2 * sum(math.prod(shape) for shape in scratch)
    lanes = others[0].shape[1]
    list_rows = -(-3 * owners * slots // (8 * lanes)) * 8
    return pl.pallas_call(
        functools.partial(string_matrix_kernel, pairs, where, per, outs, len(after)),
        out_shape=[jax.ShapeDtypeStruct((rows, blocks // outs * width), F32)] * outs,
        in_specs=[SMEM] + [VMEM] * 3 + [ANY if len(where) == 1 else VMEM] * len(others) + [ANY] * len(after),
        out_specs=[VMEM] * outs,
        scratch_shapes=[pltpu.VMEM((blocks, list_rows, lanes), F32), pltpu.VMEM((depth, depth), F32)]
        + [pltpu.VMEM(shape, BF16) for shape in scratch]
        + [pltpu.SemaphoreType.DMA((blocks,))],
        compiler_params=pltpu.CompilerParams(vmem_limit_bytes=scratch_bytes + (6 << 20)),
        cost_estimate=pl.CostEstimate(flops=flops, bytes_accessed=1 << 10, transcendentals=0),
    )(member, columns, source, integrals, *others, *after)


def stacked_kernel(count, again, *refs):
    blocks, stack_ref, copy_refs = refs[:count], refs[count + 1], refs[count + 2 :]
    rows = stack_ref.shape[0] // count
    for i, block in enumerate(blocks):
        stack_ref[i * rows : (i + 1) * rows] = block[:rows]
    for i, copy_ref in zip(again, copy_refs, strict=True):
        copy_ref[...] = blocks[i][:rows]


def stacked(blocks, again, rows, after):
    cols = blocks[0].shape[1]
    shapes = [(len(blocks) * rows, cols)] + [(rows, cols)] * len(again)
    return pl.pallas_call(
        functools.partial(stacked_kernel, len(blocks), again),
        out_shape=[jax.ShapeDtypeStruct(shape, F32) for shape in shapes],
        in_specs=[VMEM] * len(blocks) + [ANY],
        out_specs=[VMEM] * len(shapes),
        compiler_params=pltpu.CompilerParams(vmem_limit_bytes=(12 * len(blocks) * rows * cols) + (2 << 20)),
        cost_estimate=pl.CostEstimate(flops=1 << 28, bytes_accessed=1 << 10, transcendentals=0),
    )(*blocks, after)


def beta_kernel(places, nb, count, before, index_ref, *refs):
    *refs, out_ref, left_ref, right_ref = refs
    c_col, h_b = refs[: len(places)], refs[len(places) : len(places) + count]
    rows, cols = out_ref.shape
    width = nb * cols
    row = index_ref[0]
    held = sorted({d for at in places for d, _ in at})
    for chunk, h in enumerate(h_b):
        for i, d in enumerate(held):

            @pl.when(row ^ d == chunk)
            def _():
                high, low = halves(h[...])
                right_ref[i, :, :width] = high
                right_ref[i, :, width : 2 * width] = high
                right_ref[i, :, 2 * width :] = low

    for c, at in zip(c_col, places, strict=True):
        for j, (d, k) in enumerate(at):
            i = held.index(d)
            high, low = halves(c[j * rows : (j + 1) * rows])
            left_ref[i, :, k * cols : (k + 1) * cols] = high
            left_ref[i, :, width + k * cols : width + (k + 1) * cols] = low
            left_ref[i, :, 2 * width + k * cols : 2 * width + (k + 1) * cols] = high
    total = dot(left_ref[0], right_ref[0], NT)
    for i in range(1, len(held)):
        total += dot(left_ref[i], right_ref[i], NT)
    out_ref[...] = total + refs[-1][...] if before else total


def beta_part(index, c_col, places, h_b, nb, rows, cols, before=()):
    count = len({d for at in places for d, _ in at})
    operands = [*c_col, *h_b, *before]
    scratch = [(count, rows, 3 * nb * cols), (count, cols, 3 * nb * cols)]
    return pl.pallas_call(
        functools.partial(beta_kernel, places, nb, len(h_b), len(before)),
        out_shape=jax.ShapeDtypeStruct((rows, cols), F32),
        in_specs=[SMEM] + [VMEM] * len(operands),
        out_specs=VMEM,
        scratch_shapes=[pltpu.VMEM(shape, BF16) for shape in scratch],
        compiler_params=pltpu.CompilerParams(
            vmem_limit_bytes=2 * sum(math.prod(shape) for shape in scratch) + (12 << 20)
        ),
        cost_estimate=pl.CostEstimate(
            flops=100 * count * nb * rows * cols * cols, bytes_accessed=1 << 10, transcendentals=0
        ),
    )(index, *operands)


def final_kernel(count, nb, shift_ref, *refs):
    *refs, sigma_ref, correction_ref = refs
    rows, cols = sigma_ref.shape
    c_row, h_a, beta_ref, diagonal_ref = refs[:count], refs[count : count + nb], refs[-2], refs[-1]
    left = h_a[0][...]
    for h in h_a[1:]:
        left = left + h[...]
    high, low = halves(left)
    parts = [halves(c[:rows]) for c in c_row]
    high2 = joined([p[0] for p in parts], 0)
    low2 = joined([p[1] for p in parts], 0)
    total = dot(jnp.concatenate([high, low], axis=1), jnp.concatenate([high2, high2], axis=0))
    total += dot(high, low2) + beta_ref[...]
    shift = shift_ref[0]
    sigma_ref[...] = total
    correction_ref[...] = (total - shift * c_row[0][:rows]) / (diagonal_ref[...] - shift)


def final(energy_shift, c_row, h_a, beta, diagonal):
    count, nb = len(c_row), len(h_a)
    rows, cols = diagonal.shape
    operands = [*c_row, *h_a, beta, diagonal]
    return pl.pallas_call(
        functools.partial(final_kernel, count, nb),
        out_shape=[jax.ShapeDtypeStruct((rows, cols), F32)] * 2,
        in_specs=[SMEM] + [VMEM] * len(operands),
        out_specs=[VMEM] * 2,
        compiler_params=pltpu.CompilerParams(vmem_limit_bytes=(8 << 20) + 20 * count * rows * (rows + cols)),
        cost_estimate=pl.CostEstimate(
            flops=100 * count * rows * rows * cols, bytes_accessed=1 << 10, transcendentals=0
        ),
    )(energy_shift, *operands)


def shards(
    n_row,
    n_col,
    coefficients,
    diagonal,
    energy_shift,
    integrals,
    source_row,
    target_row,
    phase_row,
    source_col,
    target_col,
    phase_col,
):
    nb = n_col // n_row
    rows, cols = coefficients.shape
    pairs = integrals.shape[0]
    row, col = lax.axis_index("row"), lax.axis_index("col")
    group, member = col // nb, col % nb
    last = n_row - 1

    def members(x, k):
        return lax.ppermute(x, "col", [((c // nb) * nb + (c % nb + k) % nb, c) for c in range(n_col)])

    def rows_of(x, d):
        return lax.ppermute(x, "row", [(r, r ^ d) for r in range(n_row)])

    def lists_of(x, by):
        pairs_of = [
            (r * n_col + ((c // nb) ^ r ^ by[c % nb]) * nb + c % nb, r * n_col + c)
            for r in range(n_row)
            for c in range(n_col)
        ]
        return lax.ppermute(x, ("row", "col"), pairs_of)

    def groups(x, d):
        return lax.ppermute(x, "col", [(c, ((c // nb) ^ d) * nb + c % nb) for c in range(n_col)])

    beta = jnp.concatenate([source_col, target_col, phase_col]).astype(F32)
    owners_b, slots_b = source_col.shape
    beta_both = jnp.concatenate([beta] + [members(beta, k) for k in range(1, nb)])
    share = n_row // nb
    slots_a = source_row.shape[1]
    alpha = jnp.stack([source_row, target_row, phase_row]).astype(F32)
    alpha = lax.dynamic_slice_in_dim(alpha, member * share, share, 1)
    lists = alpha.reshape(-1, cols)
    lists = lists + 0.0 * beta_both[-1:, :1]
    lists = jnp.pad(lists, ((0, -lists.shape[0] % 8), (0, 0)))
    payload = jnp.concatenate([coefficients, lists], axis=0)
    size = 3 * owners_b
    own, swapped = [(0, k * size) for k in range(nb)], [(1, (k + 1) % nb * size) for k in range(nb)]
    if nb == 2:
        mine = lists_of(beta_both, (0, last))
        beta_lists = [mine, members(mine + 0.0 * payload[-1:, :1], 1)]
        where_b = [own + swapped, swapped + own]
    else:
        beta_lists = [lists_of(beta_both, [d] * nb) for d in (0, last)]
        where_b = [own + [(1, k * size) for k in range(nb)]]

    c_row = [payload] + [rows_of(payload, d) for d in range(1, n_row)]
    where_a = [[(d, rows) for d in range(n_row)]]
    bits = [1 << b for b in reversed(range(last.bit_length()))]
    near_by = [payload] + [groups(payload, bit) for bit in bits]

    beta_side = (beta[owners_b:].T, beta[:owners_b], integrals)
    near, far = string_matrix(member[None], *beta_side, beta_lists, where_b, pairs, cols, cols, 2)
    h_b = [near] + [rows_of(near, d) for d in range(1, last)] + [far]
    alpha_side = (alpha[1:].reshape(-1, slots_a).T, alpha[0], integrals)
    order = [0, *bits]
    more = sorted(set(range(n_row)) - set(order), key=lambda d: (d.bit_count(), d))
    again = [i for i, d in enumerate(order) if any(d == m & (m - 1) for m in more)]
    stack, *copies = stacked(near_by, again, rows, near)
    moved = {order[i]: copy for i, copy in zip(again, copies, strict=True)}
    for d in more:
        moved[d] = groups(moved[d & (d - 1)], d & -d)
    arrived = [moved[d] for d in more]
    swapped = [members(stack, k) for k in range(1, nb)]
    (part,) = string_matrix(member[None], *alpha_side, c_row, where_a, pairs, rows, rows, 1, [near])
    h_a = [part] + [members(part, k) for k in range(1, nb)]
    late = [[members(block, k) for k in range(1, nb)] for block in arrived]
    places = [[(d, k) for d in order] for k in range(nb)]
    beta_sum = beta_part(row[None], [stack, *swapped], places, h_b, nb, rows, cols)
    places = [[(d, k)] for d in more for k in range(nb)]
    c_late = [x for block, swaps in zip(arrived, late, strict=True) for x in [block, *swaps]]
    beta_sum = beta_part(row[None], c_late, places, h_b, nb, rows, cols, [beta_sum])
    return final(energy_shift, c_row, h_a, beta_sum, diagonal)


def solution(mesh):
    n_row, n_col = mesh.shape["row"], mesh.shape["col"]
    in_specs = (
        P("row", "col"),
        P("row", "col"),
        P(),
        P(),
        P("row", None),
        P("row", None),
        P("row", None),
        P("col", None),
        P("col", None),
        P("col", None),
    )
    out_specs = (P("row", "col"), P("row", "col"))
    return jax.shard_map(
        functools.partial(shards, n_row, n_col), mesh=mesh, in_specs=in_specs, out_specs=out_specs, check_vma=False
    )
```

```python
import functools
import math

import jax
import jax.numpy as jnp
from jax import lax
from jax.experimental import pallas as pl
from jax.experimental.pallas import tpu as pltpu
from jax.sharding import PartitionSpec as P

BF16 = jnp.bfloat16
F32 = jnp.float32
NN = (((1,), (0,)), ((), ()))
NT = (((1,), (1,)), ((), ()))
VMEM = pl.BlockSpec(memory_space=pltpu.VMEM)
ANY = pl.BlockSpec(memory_space=pl.ANY)
SMEM = pl.BlockSpec(memory_space=pltpu.SMEM)


def dot(x, y, dims=NN):
    return lax.dot_general(x, y, dims, preferred_element_type=F32)


def halves(x):
    high = x.astype(BF16)
    return high, (x - high.astype(F32)).astype(BF16)


def slot_of(place, pairs):
    return jnp.floor((place + 0.5) * (1.0 / pairs))


def one_hot(index, values, shape, axis):
    hit = lax.broadcasted_iota(jnp.int32, shape, axis) == index.astype(jnp.int32)
    return jnp.where(hit, values, 0.0).astype(BF16)


def joined(parts, axis):
    return parts[0] if len(parts) == 1 else jnp.concatenate(parts, axis=axis)


def fetched(sources, targets, sems):
    copies = [pltpu.make_async_copy(x, y, sems.at[i]) for i, (x, y) in enumerate(zip(sources, targets, strict=True))]
    for copy in copies:
        copy.start()
    return copies


def string_matrix_kernel(pairs, where, per, outs, after, member_ref, *refs):
    refs = iter(refs)
    columns_ref, source_ref, integrals_ref = (next(refs) for _ in range(3))
    other_refs = [next(refs) for _ in range(1 + max(array for array, _ in where[0]))]
    for _ in range(after):
        next(refs)
    out_refs = [next(refs) for _ in range(outs)]
    lists_ref, padded_ref, picked_ref, one_hot_ref, spread_ref, left_ref, sems = refs
    blocks = len(where[0])
    owners, slots = source_ref.shape
    rows, width = out_refs[0].shape
    width = width * outs // blocks
    depth = picked_ref.shape[2]
    lanes = lists_ref.shape[2]
    if len(where) == 1:
        sources = [other_refs[array].at[pl.ds(base, lists_ref.shape[1])] for array, base in where[0]]
        copies = fetched(sources, [lists_ref.at[block] for block in range(blocks)], sems)
    else:
        copies = []
        for block in range(blocks):
            choices = [other_refs[at[block][0]][pl.ds(at[block][1], lists_ref.shape[1])] for at in where]
            lists_ref[block] = jnp.where(member_ref[0] == 0, choices[0], choices[1])

    def listed(block, kind, owner):
        at = (kind * owners + owner) * slots
        if slots <= lanes:
            return lists_ref[block, at // lanes : at // lanes + 1, at % lanes : at % lanes + slots]
        return jnp.concatenate(
            [lists_ref[block, r : r + 1, :] for r in range(at // lanes, (at + slots) // lanes)], axis=1
        )

    padded_ref[...] = jnp.zeros(padded_ref.shape, F32)
    padded_ref[:pairs, :pairs] = integrals_ref[...]
    high, low = halves(padded_ref[...])
    batch = one_hot_ref.shape[0] // slots
    for first in range(0, owners, batch):
        for i in range(batch):
            place = columns_ref[:, first + i : first + i + 1]
            sign = columns_ref[:, owners + first + i : owners + first + i + 1]
            pair = place - slot_of(place, pairs) * pairs
            one_hot_ref[i * slots : (i + 1) * slots] = one_hot(pair, sign, (slots, depth), 1)
        top = dot(one_hot_ref[...], high).astype(BF16)
        rest = dot(one_hot_ref[...], low).astype(BF16)
        for i in range(batch):
            picked_ref[first + i, :slots] = top[i * slots : (i + 1) * slots]
            picked_ref[first + i, slots:] = rest[i * slots : (i + 1) * slots]
    for owner in range(owners):
        spread = one_hot(source_ref[owner : owner + 1, :], 1.0, (rows, slots), 0)
        spread_ref[owner, :, :slots] = spread
        spread_ref[owner, :, slots:] = spread
    for copy in copies:
        copy.wait()
    for first in range(0, blocks, per):
        group = range(first, first + per)
        for owner in range(owners):
            slot = slot_of(columns_ref[:, owner : owner + 1], pairs)
            picks, slots2 = [], []
            for block in group:
                place2 = listed(block, 1, owner)
                slot2 = slot_of(place2, pairs)
                slots2.append(slot2)
                picks.append(one_hot(place2 - slot2 * pairs, listed(block, 2, owner), (depth, slots), 0))
            entries = dot(picked_ref[owner], joined(picks, 1))
            same = slot == joined(slots2, 1)
            entries = jnp.concatenate(
                [jnp.where(same, entries[:slots], 0.0), jnp.where(same, entries[slots:], 0.0)], axis=0
            ).astype(BF16)
            top, rest = halves(dot(spread_ref[owner], entries))
            for i in range(per):
                left_ref[i, :rows, owner * slots : (owner + 1) * slots] = top[:, i * slots : (i + 1) * slots]
                left_ref[i, rows:, owner * slots : (owner + 1) * slots] = rest[:, i * slots : (i + 1) * slots]
        for i, block in enumerate(group):
            gathers = [one_hot(listed(block, 0, owner), 1.0, (width, slots), 0) for owner in range(owners)]
            both = dot(left_ref[i], joined(gathers, 1), NT)
            out, at = divmod(block, blocks // outs)
            out_refs[out][:, at * width : (at + 1) * width] = both[:rows] + both[rows:]


def string_matrix(member, columns, source, integrals, others, where, pairs, rows, width, outs, after=()):
    owners, slots = source.shape
    blocks = len(where[0])
    depth = -(-pairs // 256) * 256
    per = max(1, min(blocks, 512 // slots))
    batch = max(1, min(owners, 1024 // slots))
    flops = 4 * owners * slots * (depth * depth + blocks * (depth * slots + rows * slots + rows * width))
    scratch = [
        (owners, 2 * slots, depth),
        (batch * slots, depth),
        (owners, rows, 2 * slots),
        (per, 2 * rows, owners * slots),
    ]
    scratch_bytes = 2 * sum(math.prod(shape) for shape in scratch)
    lanes = others[0].shape[1]
    list_rows = -(-3 * owners * slots // (8 * lanes)) * 8
    return pl.pallas_call(
        functools.partial(string_matrix_kernel, pairs, where, per, outs, len(after)),
        out_shape=[jax.ShapeDtypeStruct((rows, blocks // outs * width), F32)] * outs,
        in_specs=[SMEM] + [VMEM] * 3 + [ANY if len(where) == 1 else VMEM] * len(others) + [ANY] * len(after),
        out_specs=[VMEM] * outs,
        scratch_shapes=[pltpu.VMEM((blocks, list_rows, lanes), F32), pltpu.VMEM((depth, depth), F32)]
        + [pltpu.VMEM(shape, BF16) for shape in scratch]
        + [pltpu.SemaphoreType.DMA((blocks,))],
        compiler_params=pltpu.CompilerParams(vmem_limit_bytes=scratch_bytes + (6 << 20)),
        cost_estimate=pl.CostEstimate(flops=flops, bytes_accessed=1 << 10, transcendentals=0),
    )(member, columns, source, integrals, *others, *after)


def stacked_kernel(count, again, *refs):
    blocks, stack_ref, copy_refs = refs[:count], refs[count + 1], refs[count + 2 :]
    rows = stack_ref.shape[0] // count
    for i, block in enumerate(blocks):
        stack_ref[i * rows : (i + 1) * rows] = block[:rows]
    for i, copy_ref in zip(again, copy_refs, strict=True):
        copy_ref[...] = blocks[i][:rows]


def stacked(blocks, again, rows, after):
    cols = blocks[0].shape[1]
    shapes = [(len(blocks) * rows, cols)] + [(rows, cols)] * len(again)
    return pl.pallas_call(
        functools.partial(stacked_kernel, len(blocks), again),
        out_shape=[jax.ShapeDtypeStruct(shape, F32) for shape in shapes],
        in_specs=[VMEM] * len(blocks) + [ANY],
        out_specs=[VMEM] * len(shapes),
        compiler_params=pltpu.CompilerParams(vmem_limit_bytes=(12 * len(blocks) * rows * cols) + (2 << 20)),
        cost_estimate=pl.CostEstimate(flops=1 << 28, bytes_accessed=1 << 10, transcendentals=0),
    )(*blocks, after)


def beta_products(places, nb, row, c_col, h_b, left_ref, right_ref):
    cols = h_b[0].shape[0]
    width = nb * cols
    rows = left_ref.shape[1]
    held = sorted({d for at in places for d, _ in at})
    for chunk, h in enumerate(h_b):
        for i, d in enumerate(held):

            @pl.when(row ^ d == chunk)
            def _():
                high, low = halves(h[...])
                right_ref[i, :, :width] = high
                right_ref[i, :, width : 2 * width] = high
                right_ref[i, :, 2 * width :] = low

    for c, at in zip(c_col, places, strict=True):
        for j, (d, k) in enumerate(at):
            i = held.index(d)
            high, low = halves(c[j * rows : (j + 1) * rows])
            left_ref[i, :, k * cols : (k + 1) * cols] = high
            left_ref[i, :, width + k * cols : width + (k + 1) * cols] = low
            left_ref[i, :, 2 * width + k * cols : 2 * width + (k + 1) * cols] = high
    total = dot(left_ref[0], right_ref[0], NT)
    for i in range(1, len(held)):
        total += dot(left_ref[i], right_ref[i], NT)
    return total


def alpha_products(left, c_row, rows):
    top, rest = halves(left)
    parts = [halves(c[:rows]) for c in c_row]
    high = joined([p[0] for p in parts], 0)
    low = joined([p[1] for p in parts], 0)
    return dot(top, high) + dot(rest, high) + dot(top, low)


def first_kernel(places, nb, count, index_ref, *refs):
    *refs, out_ref, left_ref, right_ref = refs
    n = len(places)
    c_col, h_b, c_row, part_ref = refs[:n], refs[n : n + count], refs[n + count : n + 2 * count], refs[-1]
    total = beta_products(places, nb, index_ref[0], c_col, h_b, left_ref, right_ref)
    out_ref[...] = total + alpha_products(part_ref[...], c_row, out_ref.shape[0])


def last_kernel(places, nb, count, index_ref, shift_ref, *refs):
    *refs, sigma_ref, correction_ref, left_ref, right_ref = refs
    n = len(places)
    c_col, h_b, c_row = refs[:n], refs[n : n + count], refs[n + count : n + 2 * count]
    *parts, before_ref, diagonal_ref = refs[n + 2 * count :]
    rows = sigma_ref.shape[0]
    total = before_ref[...] + beta_products(places, nb, index_ref[0], c_col, h_b, left_ref, right_ref)
    for part in parts:
        total += alpha_products(part[...], c_row, rows)
    shift = shift_ref[0]
    sigma_ref[...] = total
    correction_ref[...] = (total - shift * c_row[0][:rows]) / (diagonal_ref[...] - shift)


def product_call(kernel, places, nb, count, scalars, operands, outs, rows, cols):
    held = len({d for at in places for d, _ in at})
    scratch = [(held, rows, 3 * nb * cols), (held, cols, 3 * nb * cols)]
    return pl.pallas_call(
        functools.partial(kernel, places, nb, count),
        out_shape=outs,
        in_specs=[SMEM] * len(scalars) + [VMEM] * len(operands),
        out_specs=[VMEM] * len(outs),
        scratch_shapes=[pltpu.VMEM(shape, BF16) for shape in scratch],
        compiler_params=pltpu.CompilerParams(
            vmem_limit_bytes=2 * sum(math.prod(shape) for shape in scratch) + 10 * count * rows * cols + (10 << 20)
        ),
        cost_estimate=pl.CostEstimate(
            flops=100 * count * nb * rows * cols * cols, bytes_accessed=1 << 10, transcendentals=0
        ),
    )(*scalars, *operands)


def shards(
    n_row,
    n_col,
    coefficients,
    diagonal,
    energy_shift,
    integrals,
    source_row,
    target_row,
    phase_row,
    source_col,
    target_col,
    phase_col,
):
    nb = n_col // n_row
    rows, cols = coefficients.shape
    pairs = integrals.shape[0]
    row, col = lax.axis_index("row"), lax.axis_index("col")
    group, member = col // nb, col % nb
    last = n_row - 1

    def members(x, k):
        return lax.ppermute(x, "col", [((c // nb) * nb + (c % nb + k) % nb, c) for c in range(n_col)])

    def rows_of(x, d):
        return lax.ppermute(x, "row", [(r, r ^ d) for r in range(n_row)])

    def lists_of(x, by):
        pairs_of = [
            (r * n_col + ((c // nb) ^ r ^ by[c % nb]) * nb + c % nb, r * n_col + c)
            for r in range(n_row)
            for c in range(n_col)
        ]
        return lax.ppermute(x, ("row", "col"), pairs_of)

    def groups(x, d):
        return lax.ppermute(x, "col", [(c, ((c // nb) ^ d) * nb + c % nb) for c in range(n_col)])

    beta = jnp.concatenate([source_col, target_col, phase_col]).astype(F32)
    owners_b, slots_b = source_col.shape
    beta_both = jnp.concatenate([beta] + [members(beta, k) for k in range(1, nb)])
    share = n_row // nb
    slots_a = source_row.shape[1]
    alpha = jnp.stack([source_row, target_row, phase_row]).astype(F32)
    alpha = lax.dynamic_slice_in_dim(alpha, member * share, share, 1)
    lists = alpha.reshape(-1, cols)
    lists = lists + 0.0 * beta_both[-1:, :1]
    lists = jnp.pad(lists, ((0, -lists.shape[0] % 8), (0, 0)))
    payload = jnp.concatenate([coefficients, lists], axis=0)
    size = 3 * owners_b
    own, swapped = [(0, k * size) for k in range(nb)], [(1, (k + 1) % nb * size) for k in range(nb)]
    if nb == 2:
        mine = lists_of(beta_both, (0, last))
        beta_lists = [mine, members(mine + 0.0 * payload[-1:, :1], 1)]
        where_b = [own + swapped, swapped + own]
    else:
        beta_lists = [lists_of(beta_both, [d] * nb) for d in (0, last)]
        where_b = [own + [(1, k * size) for k in range(nb)]]

    c_row = [payload] + [rows_of(payload, d) for d in range(1, n_row)]
    where_a = [[(d, rows) for d in range(n_row)]]
    bits = [1 << b for b in reversed(range(last.bit_length()))]
    near_by = [payload] + [groups(payload, bit) for bit in bits]

    beta_side = (beta[owners_b:].T, beta[:owners_b], integrals)
    near, far = string_matrix(member[None], *beta_side, beta_lists, where_b, pairs, cols, cols, 2)
    h_b = [near] + [rows_of(near, d) for d in range(1, last)] + [far]
    alpha_side = (alpha[1:].reshape(-1, slots_a).T, alpha[0], integrals)
    order = [0, *bits]
    more = sorted(set(range(n_row)) - set(order), key=lambda d: (d.bit_count(), d))
    again = [i for i, d in enumerate(order) if any(d == m & (m - 1) for m in more)]
    stack, *copies = stacked(near_by, again, rows, near)
    moved = {order[i]: copy for i, copy in zip(again, copies, strict=True)}
    for d in more:
        moved[d] = groups(moved[d & (d - 1)], d & -d)
    arrived = [moved[d] for d in more]
    swapped = [members(stack, k) for k in range(1, nb)]
    (part,) = string_matrix(member[None], *alpha_side, c_row, where_a, pairs, rows, rows, 1, [near])
    h_a = [part] + [members(part, k) for k in range(1, nb)]
    late = [[members(block, k) for k in range(1, nb)] for block in arrived]
    index = row[None]
    whole = jax.ShapeDtypeStruct((rows, cols), F32)
    places = [[(d, k) for d in order] for k in range(nb)]
    operands = [stack, *swapped, *h_b, *c_row, part]
    (total,) = product_call(first_kernel, places, nb, n_row, [index], operands, [whole], rows, cols)
    places = [[(d, k)] for d in more for k in range(nb)]
    c_late = [x for block, swaps in zip(arrived, late, strict=True) for x in [block, *swaps]]
    operands = [*c_late, *h_b, *c_row, *h_a[1:], total, diagonal]
    return product_call(
        last_kernel, places, nb, n_row, [index, energy_shift], operands, [whole, whole], rows, cols
    )


def solution(mesh):
    n_row, n_col = mesh.shape["row"], mesh.shape["col"]
    in_specs = (
        P("row", "col"),
        P("row", "col"),
        P(),
        P(),
        P("row", None),
        P("row", None),
        P("row", None),
        P("col", None),
        P("col", None),
        P("col", None),
    )
    out_specs = (P("row", "col"), P("row", "col"))
    return jax.shard_map(
        functools.partial(shards, n_row, n_col), mesh=mesh, in_specs=in_specs, out_specs=out_specs, check_vma=False
    )
```

```python
import functools
import math

import jax
import jax.numpy as jnp
from jax import lax
from jax.experimental import pallas as pl
from jax.experimental.pallas import tpu as pltpu
from jax.sharding import PartitionSpec as P

BF16 = jnp.bfloat16
F32 = jnp.float32
NN = (((1,), (0,)), ((), ()))
NT = (((1,), (1,)), ((), ()))
VMEM = pl.BlockSpec(memory_space=pltpu.VMEM)
ANY = pl.BlockSpec(memory_space=pl.ANY)
SMEM = pl.BlockSpec(memory_space=pltpu.SMEM)


def dot(x, y, dims=NN):
    return lax.dot_general(x, y, dims, preferred_element_type=F32)


def halves(x):
    high = x.astype(BF16)
    return high, (x - high.astype(F32)).astype(BF16)


def slot_of(place, pairs):
    return jnp.floor((place + 0.5) * (1.0 / pairs))


def one_hot(index, values, shape, axis):
    hit = lax.broadcasted_iota(jnp.int32, shape, axis) == index.astype(jnp.int32)
    return jnp.where(hit, values, 0.0).astype(BF16)


def joined(parts, axis):
    return parts[0] if len(parts) == 1 else jnp.concatenate(parts, axis=axis)


def fetched(sources, targets, sems):
    copies = [pltpu.make_async_copy(x, y, sems.at[i]) for i, (x, y) in enumerate(zip(sources, targets, strict=True))]
    for copy in copies:
        copy.start()
    return copies


def string_matrix_kernel(pairs, where, per, outs, after, member_ref, *refs):
    refs = iter(refs)
    columns_ref, source_ref, integrals_ref = (next(refs) for _ in range(3))
    other_refs = [next(refs) for _ in range(1 + max(array for array, _ in where[0]))]
    for _ in range(after):
        next(refs)
    out_refs = [next(refs) for _ in range(outs)]
    lists_ref, padded_ref, picked_ref, one_hot_ref, spread_ref, left_ref, sems = refs
    blocks = len(where[0])
    owners, slots = source_ref.shape
    rows, width = out_refs[0].shape
    width = width * outs // blocks
    depth = picked_ref.shape[2]
    lanes = lists_ref.shape[2]
    if len(where) == 1:
        sources = [other_refs[array].at[pl.ds(base, lists_ref.shape[1])] for array, base in where[0]]
        copies = fetched(sources, [lists_ref.at[block] for block in range(blocks)], sems)
    else:
        copies = []
        for block in range(blocks):
            choices = [other_refs[at[block][0]][pl.ds(at[block][1], lists_ref.shape[1])] for at in where]
            lists_ref[block] = jnp.where(member_ref[0] == 0, choices[0], choices[1])

    def listed(block, kind, owner):
        at = (kind * owners + owner) * slots
        if slots <= lanes:
            return lists_ref[block, at // lanes : at // lanes + 1, at % lanes : at % lanes + slots]
        return jnp.concatenate(
            [lists_ref[block, r : r + 1, :] for r in range(at // lanes, (at + slots) // lanes)], axis=1
        )

    padded_ref[...] = jnp.zeros(padded_ref.shape, F32)
    padded_ref[:pairs, :pairs] = integrals_ref[...]
    high, low = halves(padded_ref[...])
    batch = one_hot_ref.shape[0] // slots
    for first in range(0, owners, batch):
        for i in range(batch):
            place = columns_ref[:, first + i : first + i + 1]
            sign = columns_ref[:, owners + first + i : owners + first + i + 1]
            pair = place - slot_of(place, pairs) * pairs
            one_hot_ref[i * slots : (i + 1) * slots] = one_hot(pair, sign, (slots, depth), 1)
        top = dot(one_hot_ref[...], high).astype(BF16)
        rest = dot(one_hot_ref[...], low).astype(BF16)
        for i in range(batch):
            picked_ref[first + i, :slots] = top[i * slots : (i + 1) * slots]
            picked_ref[first + i, slots:] = rest[i * slots : (i + 1) * slots]
    for owner in range(owners):
        spread = one_hot(source_ref[owner : owner + 1, :], 1.0, (rows, slots), 0)
        spread_ref[owner, :, :slots] = spread
        spread_ref[owner, :, slots:] = spread
    for copy in copies:
        copy.wait()
    for first in range(0, blocks, per):
        group = range(first, first + per)
        for owner in range(owners):
            slot = slot_of(columns_ref[:, owner : owner + 1], pairs)
            picks, slots2 = [], []
            for block in group:
                place2 = listed(block, 1, owner)
                slot2 = slot_of(place2, pairs)
                slots2.append(slot2)
                picks.append(one_hot(place2 - slot2 * pairs, listed(block, 2, owner), (depth, slots), 0))
            entries = dot(picked_ref[owner], joined(picks, 1))
            same = slot == joined(slots2, 1)
            entries = jnp.concatenate(
                [jnp.where(same, entries[:slots], 0.0), jnp.where(same, entries[slots:], 0.0)], axis=0
            ).astype(BF16)
            top, rest = halves(dot(spread_ref[owner], entries))
            for i in range(per):
                left_ref[i, :rows, owner * slots : (owner + 1) * slots] = top[:, i * slots : (i + 1) * slots]
                left_ref[i, rows:, owner * slots : (owner + 1) * slots] = rest[:, i * slots : (i + 1) * slots]
        for i, block in enumerate(group):
            gathers = [one_hot(listed(block, 0, owner), 1.0, (width, slots), 0) for owner in range(owners)]
            both = dot(left_ref[i], joined(gathers, 1), NT)
            out, at = divmod(block, blocks // outs)
            out_refs[out][:, at * width : (at + 1) * width] = both[:rows] + both[rows:]


def string_matrix(member, columns, source, integrals, others, where, pairs, rows, width, outs, after=()):
    owners, slots = source.shape
    blocks = len(where[0])
    depth = -(-pairs // 256) * 256
    per = max(1, min(blocks, 512 // slots))
    batch = max(1, min(owners, 1024 // slots))
    flops = 4 * owners * slots * (depth * depth + blocks * (depth * slots + rows * slots + rows * width))
    scratch = [
        (owners, 2 * slots, depth),
        (batch * slots, depth),
        (owners, rows, 2 * slots),
        (per, 2 * rows, owners * slots),
    ]
    scratch_bytes = 2 * sum(math.prod(shape) for shape in scratch)
    lanes = others[0].shape[1]
    list_rows = -(-3 * owners * slots // (8 * lanes)) * 8
    return pl.pallas_call(
        functools.partial(string_matrix_kernel, pairs, where, per, outs, len(after)),
        out_shape=[jax.ShapeDtypeStruct((rows, blocks // outs * width), F32)] * outs,
        in_specs=[SMEM] + [VMEM] * 3 + [ANY if len(where) == 1 else VMEM] * len(others) + [ANY] * len(after),
        out_specs=[VMEM] * outs,
        scratch_shapes=[pltpu.VMEM((blocks, list_rows, lanes), F32), pltpu.VMEM((depth, depth), F32)]
        + [pltpu.VMEM(shape, BF16) for shape in scratch]
        + [pltpu.SemaphoreType.DMA((blocks,))],
        compiler_params=pltpu.CompilerParams(vmem_limit_bytes=scratch_bytes + (6 << 20)),
        cost_estimate=pl.CostEstimate(flops=flops, bytes_accessed=1 << 10, transcendentals=0),
    )(member, columns, source, integrals, *others, *after)


def stacked_kernel(count, again, *refs):
    blocks, stack_ref, copy_refs = refs[:count], refs[count + 1], refs[count + 2 :]
    rows = stack_ref.shape[0] // count
    for i, block in enumerate(blocks):
        stack_ref[i * rows : (i + 1) * rows] = block[:rows]
    for i, copy_ref in zip(again, copy_refs, strict=True):
        copy_ref[...] = blocks[i][:rows]


def stacked(blocks, again, rows, after):
    cols = blocks[0].shape[1]
    shapes = [(len(blocks) * rows, cols)] + [(rows, cols)] * len(again)
    return pl.pallas_call(
        functools.partial(stacked_kernel, len(blocks), again),
        out_shape=[jax.ShapeDtypeStruct(shape, F32) for shape in shapes],
        in_specs=[VMEM] * len(blocks) + [ANY],
        out_specs=[VMEM] * len(shapes),
        compiler_params=pltpu.CompilerParams(vmem_limit_bytes=(12 * len(blocks) * rows * cols) + (2 << 20)),
        cost_estimate=pl.CostEstimate(flops=1 << 28, bytes_accessed=1 << 10, transcendentals=0),
    )(*blocks, after)


def beta_products(places, nb, row, c_col, h_b, left_ref, right_ref):
    cols = h_b[0].shape[0]
    width = nb * cols
    rows = left_ref.shape[1]
    held = sorted({d for at in places for d, _ in at})
    for chunk, h in enumerate(h_b):
        for i, d in enumerate(held):

            @pl.when(row ^ d == chunk)
            def _():
                high, low = halves(h[...])
                right_ref[i, :, :width] = high
                right_ref[i, :, width : 2 * width] = high
                right_ref[i, :, 2 * width :] = low

    for c, at in zip(c_col, places, strict=True):
        for j, (d, k) in enumerate(at):
            i = held.index(d)
            high, low = halves(c[j * rows : (j + 1) * rows])
            left_ref[i, :, k * cols : (k + 1) * cols] = high
            left_ref[i, :, width + k * cols : width + (k + 1) * cols] = low
            left_ref[i, :, 2 * width + k * cols : 2 * width + (k + 1) * cols] = high
    total = dot(left_ref[0], right_ref[0], NT)
    for i in range(1, len(held)):
        total += dot(left_ref[i], right_ref[i], NT)
    return total


def alpha_products(left, c_row, rows):
    top, rest = halves(left)
    parts = [halves(c[:rows]) for c in c_row]
    high = joined([p[0] for p in parts], 0)
    low = joined([p[1] for p in parts], 0)
    return dot(top, high) + dot(rest, high) + dot(top, low)


def first_kernel(places, nb, count, index_ref, *refs):
    *refs, out_ref, left_ref, right_ref = refs
    n = len(places)
    c_col, h_b, c_row, part_ref = refs[:n], refs[n : n + count], refs[n + count : n + 2 * count], refs[-1]
    total = beta_products(places, nb, index_ref[0], c_col, h_b, left_ref, right_ref)
    out_ref[...] = total + alpha_products(part_ref[...], c_row, out_ref.shape[0])


def last_kernel(places, nb, count, index_ref, shift_ref, *refs):
    *refs, sigma_ref, correction_ref, left_ref, right_ref = refs
    n = len(places)
    c_col, h_b, c_row = refs[:n], refs[n : n + count], refs[n + count : n + 2 * count]
    *parts, before_ref, diagonal_ref = refs[n + 2 * count :]
    rows = sigma_ref.shape[0]
    total = before_ref[...] + beta_products(places, nb, index_ref[0], c_col, h_b, left_ref, right_ref)
    for part in parts:
        total += alpha_products(part[...], c_row, rows)
    shift = shift_ref[0]
    sigma_ref[...] = total
    correction_ref[...] = (total - shift * c_row[0][:rows]) / (diagonal_ref[...] - shift)


def product_call(kernel, places, nb, count, scalars, operands, outs, rows, cols):
    held = len({d for at in places for d, _ in at})
    scratch = [(held, rows, 3 * nb * cols), (held, cols, 3 * nb * cols)]
    return pl.pallas_call(
        functools.partial(kernel, places, nb, count),
        out_shape=outs,
        in_specs=[SMEM] * len(scalars) + [VMEM] * len(operands),
        out_specs=[VMEM] * len(outs),
        scratch_shapes=[pltpu.VMEM(shape, BF16) for shape in scratch],
        compiler_params=pltpu.CompilerParams(
            vmem_limit_bytes=2 * sum(math.prod(shape) for shape in scratch) + 10 * count * rows * cols + (10 << 20)
        ),
        cost_estimate=pl.CostEstimate(
            flops=100 * count * nb * rows * cols * cols, bytes_accessed=1 << 10, transcendentals=0
        ),
    )(*scalars, *operands)


def shards(
    n_row,
    n_col,
    coefficients,
    diagonal,
    energy_shift,
    integrals,
    source_row,
    target_row,
    phase_row,
    source_col,
    target_col,
    phase_col,
):
    nb = n_col // n_row
    rows, cols = coefficients.shape
    pairs = integrals.shape[0]
    row, col = lax.axis_index("row"), lax.axis_index("col")
    group, member = col // nb, col % nb
    last = n_row - 1

    def members(x, k):
        return lax.ppermute(x, "col", [((c // nb) * nb + (c % nb + k) % nb, c) for c in range(n_col)])

    def rows_of(x, d):
        return lax.ppermute(x, "row", [(r, r ^ d) for r in range(n_row)])

    def lists_of(x, by):
        pairs_of = [
            (r * n_col + ((c // nb) ^ r ^ by[c % nb]) * nb + c % nb, r * n_col + c)
            for r in range(n_row)
            for c in range(n_col)
        ]
        return lax.ppermute(x, ("row", "col"), pairs_of)

    def groups(x, d):
        return lax.ppermute(x, "col", [(c, ((c // nb) ^ d) * nb + c % nb) for c in range(n_col)])

    beta = jnp.concatenate([source_col, target_col, phase_col]).astype(F32)
    owners_b, slots_b = source_col.shape
    beta_both = jnp.concatenate([beta] + [members(beta, k) for k in range(1, nb)])
    share = n_row // nb
    slots_a = source_row.shape[1]
    alpha = jnp.stack([source_row, target_row, phase_row]).astype(F32)
    alpha = lax.dynamic_slice_in_dim(alpha, member * share, share, 1)
    tie = 0.0 * jnp.tile(beta_both[-1], -(-slots_a // slots_b))[:slots_a]
    lists = (alpha + tie).reshape(-1, cols)
    lists = jnp.pad(lists, ((0, -lists.shape[0] % 8), (0, 0)))
    payload = jnp.concatenate([coefficients, lists], axis=0)
    size = 3 * owners_b
    own, swapped = [(0, k * size) for k in range(nb)], [(1, (k + 1) % nb * size) for k in range(nb)]
    if nb == 2:
        mine = lists_of(beta_both, (0, last))
        beta_lists = [mine, members(mine + 0.0 * payload[-1:, :slots_b], 1)]
        where_b = [own + swapped, swapped + own]
    else:
        beta_lists = [lists_of(beta_both, [d] * nb) for d in (0, last)]
        where_b = [own + [(1, k * size) for k in range(nb)]]

    c_row = [payload] + [rows_of(payload, d) for d in range(1, n_row)]
    where_a = [[(d, rows) for d in range(n_row)]]
    bits = [1 << b for b in reversed(range(last.bit_length()))]
    near_by = [payload] + [groups(payload, bit) for bit in bits]

    beta_side = (beta[owners_b:].T, beta[:owners_b], integrals)
    near, far = string_matrix(member[None], *beta_side, beta_lists, where_b, pairs, cols, cols, 2)
    h_b = [near] + [rows_of(near, d) for d in range(1, last)] + [far]
    alpha_side = (alpha[1:].reshape(-1, slots_a).T, alpha[0], integrals)
    order = [0, *bits]
    more = sorted(set(range(n_row)) - set(order), key=lambda d: (d.bit_count(), d))
    again = [i for i, d in enumerate(order) if any(d == m & (m - 1) for m in more)]
    stack, *copies = stacked(near_by, again, rows, near)
    moved = {order[i]: copy for i, copy in zip(again, copies, strict=True)}
    for d in more:
        moved[d] = groups(moved[d & (d - 1)], d & -d)
    arrived = [moved[d] for d in more]
    swapped = [members(stack, k) for k in range(1, nb)]
    (part,) = string_matrix(member[None], *alpha_side, c_row, where_a, pairs, rows, rows, 1, [near])
    h_a = [part] + [members(part, k) for k in range(1, nb)]
    late = [[members(block, k) for k in range(1, nb)] for block in arrived]
    index = row[None]
    whole = jax.ShapeDtypeStruct((rows, cols), F32)
    places = [[(d, k) for d in order] for k in range(nb)]
    operands = [stack, *swapped, *h_b, *c_row, part]
    (total,) = product_call(first_kernel, places, nb, n_row, [index], operands, [whole], rows, cols)
    places = [[(d, k)] for d in more for k in range(nb)]
    c_late = [x for block, swaps in zip(arrived, late, strict=True) for x in [block, *swaps]]
    operands = [*c_late, *h_b, *c_row, *h_a[1:], total, diagonal]
    return product_call(
        last_kernel, places, nb, n_row, [index, energy_shift], operands, [whole, whole], rows, cols
    )


def solution(mesh):
    n_row, n_col = mesh.shape["row"], mesh.shape["col"]
    in_specs = (
        P("row", "col"),
        P("row", "col"),
        P(),
        P(),
        P("row", None),
        P("row", None),
        P("row", None),
        P("col", None),
        P("col", None),
        P("col", None),
    )
    out_specs = (P("row", "col"), P("row", "col"))
    return jax.shard_map(
        functools.partial(shards, n_row, n_col), mesh=mesh, in_specs=in_specs, out_specs=out_specs, check_vma=False
    )
```

```python
import functools
import math

import jax
import jax.numpy as jnp
from jax import lax
from jax.experimental import pallas as pl
from jax.experimental.pallas import tpu as pltpu
from jax.sharding import PartitionSpec as P

BF16 = jnp.bfloat16
F32 = jnp.float32
NN = (((1,), (0,)), ((), ()))
NT = (((1,), (1,)), ((), ()))
VMEM = pl.BlockSpec(memory_space=pltpu.VMEM)
ANY = pl.BlockSpec(memory_space=pl.ANY)
SMEM = pl.BlockSpec(memory_space=pltpu.SMEM)


def dot(x, y, dims=NN):
    return lax.dot_general(x, y, dims, preferred_element_type=F32)


def halves(x):
    high = x.astype(BF16)
    return high, (x - high.astype(F32)).astype(BF16)


def slot_of(place, pairs):
    return jnp.floor((place + 0.5) * (1.0 / pairs))


def one_hot(index, values, shape, axis):
    hit = lax.broadcasted_iota(jnp.int32, shape, axis) == index.astype(jnp.int32)
    return jnp.where(hit, values, 0.0).astype(BF16)


def joined(parts, axis):
    return parts[0] if len(parts) == 1 else jnp.concatenate(parts, axis=axis)


def fetched(sources, targets, sems):
    copies = [pltpu.make_async_copy(x, y, sems.at[i]) for i, (x, y) in enumerate(zip(sources, targets, strict=True))]
    for copy in copies:
        copy.start()
    return copies


def string_matrix_kernel(pairs, where, per, outs, after, member_ref, *refs):
    refs = iter(refs)
    columns_ref, source_ref, integrals_ref = (next(refs) for _ in range(3))
    other_refs = [next(refs) for _ in range(1 + max(array for array, _ in where[0]))]
    for _ in range(after):
        next(refs)
    out_refs = [next(refs) for _ in range(outs)]
    lists_ref, padded_ref, picked_ref, one_hot_ref, spread_ref, left_ref, sems = refs
    blocks = len(where[0])
    owners, slots = source_ref.shape
    rows, width = out_refs[0].shape
    width = width * outs // blocks
    depth = picked_ref.shape[2]
    lanes = lists_ref.shape[2]
    if len(where) == 1:
        sources = [other_refs[array].at[pl.ds(base, lists_ref.shape[1])] for array, base in where[0]]
        copies = fetched(sources, [lists_ref.at[block] for block in range(blocks)], sems)
    else:
        copies = []
        for block in range(blocks):
            choices = [other_refs[at[block][0]][pl.ds(at[block][1], lists_ref.shape[1])] for at in where]
            lists_ref[block] = jnp.where(member_ref[0] == 0, choices[0], choices[1])

    def listed(block, kind, owner):
        at = (kind * owners + owner) * slots
        if slots <= lanes:
            return lists_ref[block, at // lanes : at // lanes + 1, at % lanes : at % lanes + slots]
        return jnp.concatenate(
            [lists_ref[block, r : r + 1, :] for r in range(at // lanes, (at + slots) // lanes)], axis=1
        )

    padded_ref[...] = jnp.zeros(padded_ref.shape, F32)
    padded_ref[:pairs, :pairs] = integrals_ref[...]
    high, low = halves(padded_ref[...])
    batch = one_hot_ref.shape[0] // slots
    for first in range(0, owners, batch):
        for i in range(batch):
            place = columns_ref[:, first + i : first + i + 1]
            sign = columns_ref[:, owners + first + i : owners + first + i + 1]
            pair = place - slot_of(place, pairs) * pairs
            one_hot_ref[i * slots : (i + 1) * slots] = one_hot(pair, sign, (slots, depth), 1)
        top = dot(one_hot_ref[...], high).astype(BF16)
        rest = dot(one_hot_ref[...], low).astype(BF16)
        for i in range(batch):
            picked_ref[first + i, :slots] = top[i * slots : (i + 1) * slots]
            picked_ref[first + i, slots:] = rest[i * slots : (i + 1) * slots]
    for owner in range(owners):
        spread = one_hot(source_ref[owner : owner + 1, :], 1.0, (rows, slots), 0)
        spread_ref[owner, :, :slots] = spread
        spread_ref[owner, :, slots:] = spread
    for copy in copies:
        copy.wait()
    for first in range(0, blocks, per):
        group = range(first, first + per)
        for owner in range(owners):
            slot = slot_of(columns_ref[:, owner : owner + 1], pairs)
            picks, slots2 = [], []
            for block in group:
                place2 = listed(block, 1, owner)
                slot2 = slot_of(place2, pairs)
                slots2.append(slot2)
                picks.append(one_hot(place2 - slot2 * pairs, listed(block, 2, owner), (depth, slots), 0))
            entries = dot(picked_ref[owner], joined(picks, 1))
            same = slot == joined(slots2, 1)
            entries = jnp.concatenate(
                [jnp.where(same, entries[:slots], 0.0), jnp.where(same, entries[slots:], 0.0)], axis=0
            ).astype(BF16)
            top, rest = halves(dot(spread_ref[owner], entries))
            for i in range(per):
                left_ref[i, :rows, owner * slots : (owner + 1) * slots] = top[:, i * slots : (i + 1) * slots]
                left_ref[i, rows:, owner * slots : (owner + 1) * slots] = rest[:, i * slots : (i + 1) * slots]
        for i, block in enumerate(group):
            gathers = [one_hot(listed(block, 0, owner), 1.0, (width, slots), 0) for owner in range(owners)]
            both = dot(left_ref[i], joined(gathers, 1), NT)
            out, at = divmod(block, blocks // outs)
            out_refs[out][:, at * width : (at + 1) * width] = both[:rows] + both[rows:]


def string_matrix(member, columns, source, integrals, others, where, pairs, rows, width, outs, after=()):
    owners, slots = source.shape
    blocks = len(where[0])
    depth = -(-pairs // 256) * 256
    per = max(1, min(blocks, 4, (1024 if slots < 512 else 512) // slots))
    batch = max(1, min(owners, 1024 // slots))
    flops = 4 * owners * slots * (depth * depth + blocks * (depth * slots + rows * slots + rows * width))
    scratch = [
        (owners, 2 * slots, depth),
        (batch * slots, depth),
        (owners, rows, 2 * slots),
        (per, 2 * rows, owners * slots),
    ]
    scratch_bytes = 2 * sum(math.prod(shape) for shape in scratch)
    lanes = others[0].shape[1]
    list_rows = -(-3 * owners * slots // (8 * lanes)) * 8
    return pl.pallas_call(
        functools.partial(string_matrix_kernel, pairs, where, per, outs, len(after)),
        out_shape=[jax.ShapeDtypeStruct((rows, blocks // outs * width), F32)] * outs,
        in_specs=[SMEM] + [VMEM] * 3 + [ANY if len(where) == 1 else VMEM] * len(others) + [ANY] * len(after),
        out_specs=[VMEM] * outs,
        scratch_shapes=[pltpu.VMEM((blocks, list_rows, lanes), F32), pltpu.VMEM((depth, depth), F32)]
        + [pltpu.VMEM(shape, BF16) for shape in scratch]
        + [pltpu.SemaphoreType.DMA((blocks,))],
        compiler_params=pltpu.CompilerParams(vmem_limit_bytes=scratch_bytes + (6 << 20)),
        cost_estimate=pl.CostEstimate(flops=flops, bytes_accessed=1 << 10, transcendentals=0),
    )(member, columns, source, integrals, *others, *after)


def stacked_kernel(count, again, *refs):
    blocks, stack_ref, copy_refs = refs[:count], refs[count + 1], refs[count + 2 :]
    rows = stack_ref.shape[0] // count
    for i, block in enumerate(blocks):
        stack_ref[i * rows : (i + 1) * rows] = block[:rows]
    for i, copy_ref in zip(again, copy_refs, strict=True):
        copy_ref[...] = blocks[i][:rows]


def stacked(blocks, again, rows, after):
    cols = blocks[0].shape[1]
    shapes = [(len(blocks) * rows, cols)] + [(rows, cols)] * len(again)
    return pl.pallas_call(
        functools.partial(stacked_kernel, len(blocks), again),
        out_shape=[jax.ShapeDtypeStruct(shape, F32) for shape in shapes],
        in_specs=[VMEM] * len(blocks) + [ANY],
        out_specs=[VMEM] * len(shapes),
        compiler_params=pltpu.CompilerParams(vmem_limit_bytes=(12 * len(blocks) * rows * cols) + (2 << 20)),
        cost_estimate=pl.CostEstimate(flops=1 << 28, bytes_accessed=1 << 10, transcendentals=0),
    )(*blocks, after)


def beta_products(places, nb, row, c_col, h_b, left_ref, right_ref):
    cols = h_b[0].shape[0]
    width = nb * cols
    rows = left_ref.shape[1]
    held = sorted({d for at in places for d, _ in at})
    for chunk, h in enumerate(h_b):
        for i, d in enumerate(held):

            @pl.when(row ^ d == chunk)
            def _():
                high, low = halves(h[...])
                right_ref[i, :, :width] = high
                right_ref[i, :, width : 2 * width] = high
                right_ref[i, :, 2 * width :] = low

    for c, at in zip(c_col, places, strict=True):
        for j, (d, k) in enumerate(at):
            i = held.index(d)
            high, low = halves(c[j * rows : (j + 1) * rows])
            left_ref[i, :, k * cols : (k + 1) * cols] = high
            left_ref[i, :, width + k * cols : width + (k + 1) * cols] = low
            left_ref[i, :, 2 * width + k * cols : 2 * width + (k + 1) * cols] = high
    total = dot(left_ref[0], right_ref[0], NT)
    for i in range(1, len(held)):
        total += dot(left_ref[i], right_ref[i], NT)
    return total


def alpha_products(left, c_row, rows):
    top, rest = halves(left)
    parts = [halves(c[:rows]) for c in c_row]
    high = joined([p[0] for p in parts], 0)
    low = joined([p[1] for p in parts], 0)
    return dot(top, high) + dot(rest, high) + dot(top, low)


def first_kernel(places, nb, count, index_ref, *refs):
    *refs, out_ref, left_ref, right_ref = refs
    n = len(places)
    c_col, h_b, c_row, part_ref = refs[:n], refs[n : n + count], refs[n + count : n + 2 * count], refs[-1]
    total = beta_products(places, nb, index_ref[0], c_col, h_b, left_ref, right_ref)
    out_ref[...] = total + alpha_products(part_ref[...], c_row, out_ref.shape[0])


def last_kernel(places, nb, count, index_ref, shift_ref, *refs):
    *refs, sigma_ref, correction_ref, left_ref, right_ref = refs
    n = len(places)
    c_col, h_b, c_row = refs[:n], refs[n : n + count], refs[n + count : n + 2 * count]
    *parts, before_ref, diagonal_ref = refs[n + 2 * count :]
    rows = sigma_ref.shape[0]
    total = before_ref[...] + beta_products(places, nb, index_ref[0], c_col, h_b, left_ref, right_ref)
    for part in parts:
        total += alpha_products(part[...], c_row, rows)
    shift = shift_ref[0]
    sigma_ref[...] = total
    correction_ref[...] = (total - shift * c_row[0][:rows]) / (diagonal_ref[...] - shift)


def product_call(kernel, places, nb, count, scalars, operands, outs, rows, cols):
    held = len({d for at in places for d, _ in at})
    scratch = [(held, rows, 3 * nb * cols), (held, cols, 3 * nb * cols)]
    return pl.pallas_call(
        functools.partial(kernel, places, nb, count),
        out_shape=outs,
        in_specs=[SMEM] * len(scalars) + [VMEM] * len(operands),
        out_specs=[VMEM] * len(outs),
        scratch_shapes=[pltpu.VMEM(shape, BF16) for shape in scratch],
        compiler_params=pltpu.CompilerParams(
            vmem_limit_bytes=2 * sum(math.prod(shape) for shape in scratch) + 10 * count * rows * cols + (10 << 20)
        ),
        cost_estimate=pl.CostEstimate(
            flops=100 * count * nb * rows * cols * cols, bytes_accessed=1 << 10, transcendentals=0
        ),
    )(*scalars, *operands)


def shards(
    n_row,
    n_col,
    coefficients,
    diagonal,
    energy_shift,
    integrals,
    source_row,
    target_row,
    phase_row,
    source_col,
    target_col,
    phase_col,
):
    nb = n_col // n_row
    rows, cols = coefficients.shape
    pairs = integrals.shape[0]
    row, col = lax.axis_index("row"), lax.axis_index("col")
    group, member = col // nb, col % nb
    last = n_row - 1

    def members(x, k):
        return lax.ppermute(x, "col", [((c // nb) * nb + (c % nb + k) % nb, c) for c in range(n_col)])

    def rows_of(x, d):
        return lax.ppermute(x, "row", [(r, r ^ d) for r in range(n_row)])

    def lists_of(x, by):
        pairs_of = [
            (r * n_col + ((c // nb) ^ r ^ by[c % nb]) * nb + c % nb, r * n_col + c)
            for r in range(n_row)
            for c in range(n_col)
        ]
        return lax.ppermute(x, ("row", "col"), pairs_of)

    def groups(x, d):
        return lax.ppermute(x, "col", [(c, ((c // nb) ^ d) * nb + c % nb) for c in range(n_col)])

    beta = jnp.concatenate([source_col, target_col, phase_col]).astype(F32)
    owners_b, slots_b = source_col.shape
    beta_both = jnp.concatenate([beta] + [members(beta, k) for k in range(1, nb)])
    share = n_row // nb
    slots_a = source_row.shape[1]
    alpha = jnp.stack([source_row, target_row, phase_row]).astype(F32)
    alpha = lax.dynamic_slice_in_dim(alpha, member * share, share, 1)
    tie = 0.0 * jnp.tile(beta_both[-1], -(-slots_a // slots_b))[:slots_a]
    lists = (alpha + tie).reshape(-1, cols)
    lists = jnp.pad(lists, ((0, -lists.shape[0] % 8), (0, 0)))
    payload = jnp.concatenate([coefficients, lists], axis=0)
    size = 3 * owners_b
    own, swapped = [(0, k * size) for k in range(nb)], [(1, (k + 1) % nb * size) for k in range(nb)]
    if nb == 2:
        mine = lists_of(beta_both, (0, last))
        beta_lists = [mine, members(mine + 0.0 * payload[-1:, :slots_b], 1)]
        where_b = [own + swapped, swapped + own]
    else:
        beta_lists = [lists_of(beta_both, [d] * nb) for d in (0, last)]
        where_b = [own + [(1, k * size) for k in range(nb)]]

    c_row = [payload] + [rows_of(payload, d) for d in range(1, n_row)]
    where_a = [[(d, rows) for d in range(n_row)]]
    bits = [1 << b for b in reversed(range(last.bit_length()))]
    near_by = [payload] + [groups(payload, bit) for bit in bits]

    beta_side = (beta[owners_b:].T, beta[:owners_b], integrals)
    near, far = string_matrix(member[None], *beta_side, beta_lists, where_b, pairs, cols, cols, 2)
    h_b = [near] + [rows_of(near, d) for d in range(1, last)] + [far]
    alpha_side = (alpha[1:].reshape(-1, slots_a).T, alpha[0], integrals)
    order = [0, *bits]
    more = sorted(set(range(n_row)) - set(order), key=lambda d: (d.bit_count(), d))
    again = [i for i, d in enumerate(order) if any(d == m & (m - 1) for m in more)]
    stack, *copies = stacked(near_by, again, rows, near)
    moved = {order[i]: copy for i, copy in zip(again, copies, strict=True)}
    for d in more:
        moved[d] = groups(moved[d & (d - 1)], d & -d)
    arrived = [moved[d] for d in more]
    swapped = [members(stack, k) for k in range(1, nb)]
    (part,) = string_matrix(member[None], *alpha_side, c_row, where_a, pairs, rows, rows, 1, [near])
    h_a = [part] + [members(part, k) for k in range(1, nb)]
    late = [[members(block, k) for k in range(1, nb)] for block in arrived]
    index = row[None]
    whole = jax.ShapeDtypeStruct((rows, cols), F32)
    places = [[(d, k) for d in order] for k in range(nb)]
    operands = [stack, *swapped, *h_b, *c_row, part]
    (total,) = product_call(first_kernel, places, nb, n_row, [index], operands, [whole], rows, cols)
    places = [[(d, k)] for d in more for k in range(nb)]
    c_late = [x for block, swaps in zip(arrived, late, strict=True) for x in [block, *swaps]]
    operands = [*c_late, *h_b, *c_row, *h_a[1:], total, diagonal]
    return product_call(
        last_kernel, places, nb, n_row, [index, energy_shift], operands, [whole, whole], rows, cols
    )


def solution(mesh):
    n_row, n_col = mesh.shape["row"], mesh.shape["col"]
    in_specs = (
        P("row", "col"),
        P("row", "col"),
        P(),
        P(),
        P("row", None),
        P("row", None),
        P("row", None),
        P("col", None),
        P("col", None),
        P("col", None),
    )
    out_specs = (P("row", "col"), P("row", "col"))
    return jax.shard_map(
        functools.partial(shards, n_row, n_col), mesh=mesh, in_specs=in_specs, out_specs=out_specs, check_vma=False
    )
```

```python
import functools
import math

import jax
import jax.numpy as jnp
from jax import lax
from jax.experimental import pallas as pl
from jax.experimental.pallas import tpu as pltpu
from jax.sharding import PartitionSpec as P

BF16 = jnp.bfloat16
F32 = jnp.float32
NN = (((1,), (0,)), ((), ()))
NT = (((1,), (1,)), ((), ()))
VMEM = pl.BlockSpec(memory_space=pltpu.VMEM)
ANY = pl.BlockSpec(memory_space=pl.ANY)
SMEM = pl.BlockSpec(memory_space=pltpu.SMEM)


def dot(x, y, dims=NN):
    return lax.dot_general(x, y, dims, preferred_element_type=F32)


def halves(x):
    high = x.astype(BF16)
    return high, (x - high.astype(F32)).astype(BF16)


def slot_of(place, pairs):
    return jnp.floor((place + 0.5) * (1.0 / pairs))


def one_hot(index, values, shape, axis):
    hit = lax.broadcasted_iota(jnp.int32, shape, axis) == index.astype(jnp.int32)
    return jnp.where(hit, values, 0.0).astype(BF16)


def joined(parts, axis):
    return parts[0] if len(parts) == 1 else jnp.concatenate(parts, axis=axis)


def fetched(sources, targets, sems):
    copies = [pltpu.make_async_copy(x, y, sems.at[i]) for i, (x, y) in enumerate(zip(sources, targets, strict=True))]
    for copy in copies:
        copy.start()
    return copies


def string_matrix_kernel(pairs, where, per, outs, after, member_ref, *refs):
    refs = iter(refs)
    columns_ref, source_ref, integrals_ref = (next(refs) for _ in range(3))
    other_refs = [next(refs) for _ in range(1 + max(array for array, _ in where[0]))]
    for _ in range(after):
        next(refs)
    out_refs = [next(refs) for _ in range(outs)]
    lists_ref, padded_ref, picked_ref, one_hot_ref, spread_ref, left_ref, sems = refs
    blocks = len(where[0])
    owners, slots = source_ref.shape
    rows, width = out_refs[0].shape
    width = width * outs // blocks
    depth = picked_ref.shape[2]
    lanes = lists_ref.shape[2]
    if len(where) == 1:
        sources = [other_refs[array].at[pl.ds(base, lists_ref.shape[1])] for array, base in where[0]]
        copies = fetched(sources, [lists_ref.at[block] for block in range(blocks)], sems)
    else:
        copies = []
        for block in range(blocks):
            choices = [other_refs[at[block][0]][pl.ds(at[block][1], lists_ref.shape[1])] for at in where]
            lists_ref[block] = jnp.where(member_ref[0] == 0, choices[0], choices[1])

    def listed(block, kind, owner):
        at = (kind * owners + owner) * slots
        if slots <= lanes:
            return lists_ref[block, at // lanes : at // lanes + 1, at % lanes : at % lanes + slots]
        return jnp.concatenate(
            [lists_ref[block, r : r + 1, :] for r in range(at // lanes, (at + slots) // lanes)], axis=1
        )

    padded_ref[...] = jnp.zeros(padded_ref.shape, F32)
    padded_ref[:pairs, :pairs] = integrals_ref[...]
    high, low = halves(padded_ref[...])
    batch = one_hot_ref.shape[0] // slots
    for first in range(0, owners, batch):
        for i in range(batch):
            place = columns_ref[:, first + i : first + i + 1]
            sign = columns_ref[:, owners + first + i : owners + first + i + 1]
            pair = place - slot_of(place, pairs) * pairs
            one_hot_ref[i * slots : (i + 1) * slots] = one_hot(pair, sign, (slots, depth), 1)
        top = dot(one_hot_ref[...], high).astype(BF16)
        rest = dot(one_hot_ref[...], low).astype(BF16)
        for i in range(batch):
            picked_ref[first + i, :slots] = top[i * slots : (i + 1) * slots]
            picked_ref[first + i, slots:] = rest[i * slots : (i + 1) * slots]
    for owner in range(owners):
        spread = one_hot(source_ref[owner : owner + 1, :], 1.0, (rows, slots), 0)
        spread_ref[owner, :, :slots] = spread
        spread_ref[owner, :, slots:] = spread
    for copy in copies:
        copy.wait()
    for first in range(0, blocks, per):
        group = range(first, first + per)
        for owner in range(owners):
            slot = slot_of(columns_ref[:, owner : owner + 1], pairs)
            picks, slots2 = [], []
            for block in group:
                place2 = listed(block, 1, owner)
                slot2 = slot_of(place2, pairs)
                slots2.append(slot2)
                picks.append(one_hot(place2 - slot2 * pairs, listed(block, 2, owner), (depth, slots), 0))
            entries = dot(picked_ref[owner], joined(picks, 1))
            same = slot == joined(slots2, 1)
            entries = jnp.concatenate(
                [jnp.where(same, entries[:slots], 0.0), jnp.where(same, entries[slots:], 0.0)], axis=0
            ).astype(BF16)
            top, rest = halves(dot(spread_ref[owner], entries))
            for i in range(per):
                left_ref[i, :rows, owner * slots : (owner + 1) * slots] = top[:, i * slots : (i + 1) * slots]
                left_ref[i, rows:, owner * slots : (owner + 1) * slots] = rest[:, i * slots : (i + 1) * slots]
        for i, block in enumerate(group):
            gathers = [one_hot(listed(block, 0, owner), 1.0, (width, slots), 0) for owner in range(owners)]
            both = dot(left_ref[i], joined(gathers, 1), NT)
            out, at = divmod(block, blocks // outs)
            out_refs[out][:, at * width : (at + 1) * width] = both[:rows] + both[rows:]


def string_matrix(member, columns, source, integrals, others, where, pairs, rows, width, outs, after=()):
    owners, slots = source.shape
    blocks = len(where[0])
    depth = -(-pairs // 256) * 256
    per = max(1, min(blocks, 4, (1024 if slots < 512 else 512) // slots))
    batch = max(1, min(owners, 512 // slots))
    flops = 4 * owners * slots * (depth * depth + blocks * (depth * slots + rows * slots + rows * width))
    scratch = [
        (owners, 2 * slots, depth),
        (batch * slots, depth),
        (owners, rows, 2 * slots),
        (per, 2 * rows, owners * slots),
    ]
    scratch_bytes = 2 * sum(math.prod(shape) for shape in scratch)
    lanes = others[0].shape[1]
    list_rows = -(-3 * owners * slots // (8 * lanes)) * 8
    return pl.pallas_call(
        functools.partial(string_matrix_kernel, pairs, where, per, outs, len(after)),
        out_shape=[jax.ShapeDtypeStruct((rows, blocks // outs * width), F32)] * outs,
        in_specs=[SMEM] + [VMEM] * 3 + [ANY if len(where) == 1 else VMEM] * len(others) + [ANY] * len(after),
        out_specs=[VMEM] * outs,
        scratch_shapes=[pltpu.VMEM((blocks, list_rows, lanes), F32), pltpu.VMEM((depth, depth), F32)]
        + [pltpu.VMEM(shape, BF16) for shape in scratch]
        + [pltpu.SemaphoreType.DMA((blocks,))],
        compiler_params=pltpu.CompilerParams(vmem_limit_bytes=scratch_bytes + (6 << 20)),
        cost_estimate=pl.CostEstimate(flops=flops, bytes_accessed=1 << 10, transcendentals=0),
    )(member, columns, source, integrals, *others, *after)


def stacked_kernel(count, again, *refs):
    blocks, stack_ref, copy_refs = refs[:count], refs[count + 1], refs[count + 2 :]
    rows = stack_ref.shape[0] // count
    for i, block in enumerate(blocks):
        stack_ref[i * rows : (i + 1) * rows] = block[:rows]
    for i, copy_ref in zip(again, copy_refs, strict=True):
        copy_ref[...] = blocks[i][:rows]


def stacked(blocks, again, rows, after):
    cols = blocks[0].shape[1]
    shapes = [(len(blocks) * rows, cols)] + [(rows, cols)] * len(again)
    return pl.pallas_call(
        functools.partial(stacked_kernel, len(blocks), again),
        out_shape=[jax.ShapeDtypeStruct(shape, F32) for shape in shapes],
        in_specs=[VMEM] * len(blocks) + [ANY],
        out_specs=[VMEM] * len(shapes),
        compiler_params=pltpu.CompilerParams(vmem_limit_bytes=(12 * len(blocks) * rows * cols) + (2 << 20)),
        cost_estimate=pl.CostEstimate(flops=1 << 28, bytes_accessed=1 << 10, transcendentals=0),
    )(*blocks, after)


def beta_products(places, nb, row, c_col, h_b, left_ref, right_ref):
    cols = h_b[0].shape[0]
    width = nb * cols
    rows = left_ref.shape[1]
    held = sorted({d for at in places for d, _ in at})
    for chunk, h in enumerate(h_b):
        for i, d in enumerate(held):

            @pl.when(row ^ d == chunk)
            def _():
                high, low = halves(h[...])
                right_ref[i, :, :width] = high
                right_ref[i, :, width : 2 * width] = high
                right_ref[i, :, 2 * width :] = low

    for c, at in zip(c_col, places, strict=True):
        for j, (d, k) in enumerate(at):
            i = held.index(d)
            high, low = halves(c[j * rows : (j + 1) * rows])
            left_ref[i, :, k * cols : (k + 1) * cols] = high
            left_ref[i, :, width + k * cols : width + (k + 1) * cols] = low
            left_ref[i, :, 2 * width + k * cols : 2 * width + (k + 1) * cols] = high
    total = dot(left_ref[0], right_ref[0], NT)
    for i in range(1, len(held)):
        total += dot(left_ref[i], right_ref[i], NT)
    return total


def alpha_products(left, c_row, rows):
    top, rest = halves(left)
    parts = [halves(c[:rows]) for c in c_row]
    high = joined([p[0] for p in parts], 0)
    low = joined([p[1] for p in parts], 0)
    return dot(top, high) + dot(rest, high) + dot(top, low)


def first_kernel(places, nb, count, index_ref, *refs):
    *refs, out_ref, left_ref, right_ref = refs
    n = len(places)
    c_col, h_b, c_row, part_ref = refs[:n], refs[n : n + count], refs[n + count : n + 2 * count], refs[-1]
    total = beta_products(places, nb, index_ref[0], c_col, h_b, left_ref, right_ref)
    out_ref[...] = total + alpha_products(part_ref[...], c_row, out_ref.shape[0])


def last_kernel(places, nb, count, index_ref, shift_ref, *refs):
    *refs, sigma_ref, correction_ref, left_ref, right_ref = refs
    n = len(places)
    c_col, h_b, c_row = refs[:n], refs[n : n + count], refs[n + count : n + 2 * count]
    *parts, before_ref, diagonal_ref = refs[n + 2 * count :]
    rows = sigma_ref.shape[0]
    total = before_ref[...] + beta_products(places, nb, index_ref[0], c_col, h_b, left_ref, right_ref)
    for part in parts:
        total += alpha_products(part[...], c_row, rows)
    shift = shift_ref[0]
    sigma_ref[...] = total
    correction_ref[...] = (total - shift * c_row[0][:rows]) / (diagonal_ref[...] - shift)


def product_call(kernel, places, nb, count, scalars, operands, outs, rows, cols):
    held = len({d for at in places for d, _ in at})
    scratch = [(held, rows, 3 * nb * cols), (held, cols, 3 * nb * cols)]
    return pl.pallas_call(
        functools.partial(kernel, places, nb, count),
        out_shape=outs,
        in_specs=[SMEM] * len(scalars) + [VMEM] * len(operands),
        out_specs=[VMEM] * len(outs),
        scratch_shapes=[pltpu.VMEM(shape, BF16) for shape in scratch],
        compiler_params=pltpu.CompilerParams(
            vmem_limit_bytes=2 * sum(math.prod(shape) for shape in scratch) + 10 * count * rows * cols + (10 << 20)
        ),
        cost_estimate=pl.CostEstimate(
            flops=100 * count * nb * rows * cols * cols, bytes_accessed=1 << 10, transcendentals=0
        ),
    )(*scalars, *operands)


def shards(
    n_row,
    n_col,
    coefficients,
    diagonal,
    energy_shift,
    integrals,
    source_row,
    target_row,
    phase_row,
    source_col,
    target_col,
    phase_col,
):
    nb = n_col // n_row
    rows, cols = coefficients.shape
    pairs = integrals.shape[0]
    row, col = lax.axis_index("row"), lax.axis_index("col")
    group, member = col // nb, col % nb
    last = n_row - 1

    def members(x, k):
        return lax.ppermute(x, "col", [((c // nb) * nb + (c % nb + k) % nb, c) for c in range(n_col)])

    def rows_of(x, d):
        return lax.ppermute(x, "row", [(r, r ^ d) for r in range(n_row)])

    def lists_of(x, by):
        pairs_of = [
            (r * n_col + ((c // nb) ^ r ^ by[c % nb]) * nb + c % nb, r * n_col + c)
            for r in range(n_row)
            for c in range(n_col)
        ]
        return lax.ppermute(x, ("row", "col"), pairs_of)

    def groups(x, d):
        return lax.ppermute(x, "col", [(c, ((c // nb) ^ d) * nb + c % nb) for c in range(n_col)])

    beta = jnp.concatenate([source_col, target_col, phase_col]).astype(F32)
    owners_b, slots_b = source_col.shape
    beta_both = jnp.concatenate([beta] + [members(beta, k) for k in range(1, nb)])
    share = n_row // nb
    slots_a = source_row.shape[1]
    alpha = jnp.stack([source_row, target_row, phase_row]).astype(F32)
    alpha = lax.dynamic_slice_in_dim(alpha, member * share, share, 1)
    tie = 0.0 * jnp.tile(beta_both[-1], -(-slots_a // slots_b))[:slots_a]
    lists = (alpha + tie).reshape(-1, cols)
    lists = jnp.pad(lists, ((0, -lists.shape[0] % 8), (0, 0)))
    payload = jnp.concatenate([coefficients, lists], axis=0)
    size = 3 * owners_b
    own, swapped = [(0, k * size) for k in range(nb)], [(1, (k + 1) % nb * size) for k in range(nb)]
    if nb == 2:
        mine = lists_of(beta_both, (0, last))
        beta_lists = [mine, members(mine + 0.0 * payload[-1:, :slots_b], 1)]
        where_b = [own + swapped, swapped + own]
    else:
        beta_lists = [lists_of(beta_both, [d] * nb) for d in (0, last)]
        where_b = [own + [(1, k * size) for k in range(nb)]]

    c_row = [payload] + [rows_of(payload, d) for d in range(1, n_row)]
    where_a = [[(d, rows) for d in range(n_row)]]
    bits = [1 << b for b in reversed(range(last.bit_length()))]
    near_by = [payload] + [groups(payload, bit) for bit in bits]

    beta_side = (beta[owners_b:].T, beta[:owners_b], integrals)
    near, far = string_matrix(member[None], *beta_side, beta_lists, where_b, pairs, cols, cols, 2)
    h_b = [near] + [rows_of(near, d) for d in range(1, last)] + [far]
    alpha_side = (alpha[1:].reshape(-1, slots_a).T, alpha[0], integrals)
    order = [0, *bits]
    more = sorted(set(range(n_row)) - set(order), key=lambda d: (d.bit_count(), d))
    again = [i for i, d in enumerate(order) if any(d == m & (m - 1) for m in more)]
    stack, *copies = stacked(near_by, again, rows, near)
    moved = {order[i]: copy for i, copy in zip(again, copies, strict=True)}
    for d in more:
        moved[d] = groups(moved[d & (d - 1)], d & -d)
    arrived = [moved[d] for d in more]
    swapped = [members(stack, k) for k in range(1, nb)]
    (part,) = string_matrix(member[None], *alpha_side, c_row, where_a, pairs, rows, rows, 1, [near])
    h_a = [part] + [members(part, k) for k in range(1, nb)]
    late = [[members(block, k) for k in range(1, nb)] for block in arrived]
    index = row[None]
    whole = jax.ShapeDtypeStruct((rows, cols), F32)
    places = [[(d, k) for d in order] for k in range(nb)]
    operands = [stack, *swapped, *h_b, *c_row, part]
    (total,) = product_call(first_kernel, places, nb, n_row, [index], operands, [whole], rows, cols)
    places = [[(d, k)] for d in more for k in range(nb)]
    c_late = [x for block, swaps in zip(arrived, late, strict=True) for x in [block, *swaps]]
    operands = [*c_late, *h_b, *c_row, *h_a[1:], total, diagonal]
    return product_call(
        last_kernel, places, nb, n_row, [index, energy_shift], operands, [whole, whole], rows, cols
    )


def solution(mesh):
    n_row, n_col = mesh.shape["row"], mesh.shape["col"]
    in_specs = (
        P("row", "col"),
        P("row", "col"),
        P(),
        P(),
        P("row", None),
        P("row", None),
        P("row", None),
        P("col", None),
        P("col", None),
        P("col", None),
    )
    out_specs = (P("row", "col"), P("row", "col"))
    return jax.shard_map(
        functools.partial(shards, n_row, n_col), mesh=mesh, in_specs=in_specs, out_specs=out_specs, check_vma=False
    )
```
